32 devices in a mesh: study: 2 (over x), vol: 8 (over z, y), tile: 2 (over core).
Axes of the slice: x: 2, y: 2, z: 4, core: 2. Of those that a mesh axis runs over, the one named last changes fastest.
Arguments:
- spectra: bfloat16 [16, 4, 768, 2048], P(('study', 'vol'), None, 'tile'), parts along dimension 0, may hold values from -6 to 6
- block_scales: float32 [16, 4, 768, 16], P(('study', 'vol'), None, 'tile'), parts along dimension 0, may hold values from 0.3 to 3
- retina_blocks: int32 [12, 2], P(('study', 'tile')), parts along dimension 0, may hold values from 0 to 3, as said below
- quality_block: int32 [16, 6], P(('study', 'vol'), 'tile'), parts along dimension 0, may hold values from 0 to 3, as said below
- quality_bias: float32 [16, 6], P(('study', 'vol'), 'tile'), parts along dimension 0, may hold values from -110 to 160
Outputs:
- angiogram: float32 [1024, 768], P(('study', 'vol'), 'tile'), parts along dimension 0
- joined_structure: float32 [1024, 768], P(('study', 'vol'), 'tile'), parts along dimension 0
- spread_map: float32 [1024, 768], P(('study', 'vol'), 'tile'), parts along dimension 0
The draws below stay inside these ranges and needn't reach their ends.
There are 2 independent parts, one for each index of `study`. The reference program is written for one: setup_inputs(seed, part) draws one part's arguments, and reference() takes and returns one part's arrays. A program takes and returns all parts, laid end to end along the dimension named above; each array names one. Nothing has to cross between parts.
Inputs may be any that keep to these rules, and one draw needn't show every extreme that they name: retina_blocks[j,0] <= retina_blocks[j,1]. quality_block[v,j] lies between retina_blocks[j,0] and retina_blocks[j,1].
All inputs are finite; a program needn't handle non-finite values.
Results may differ from the reference program's by a relative error of at most 0.0015.
Values sent between devices are 32-bit elements; how exact they have to be, the bound alone decides.
No kernel may reach another device: no remote copies, remote signals or barrier semaphores. Data moves between devices by JAX's collectives and lax.ppermute only.
A program may use at most 128 MiB of HBM per device.

```python
import math
import jax
import jax.numpy as jnp
from jax import lax

K = 2048
DEPTH = 512
BANDS = 4
REPEATS = 4
DBLK = 128
ABLK = 128
SB = 128
ALINES = 768
VOLS = 8
ABLKS = 6
KB = 16
NDB = 4


def draw_pattern(key):
    key_first = jax.random.fold_in(key, 101)
    key_last = jax.random.fold_in(key, 102)
    key_zero = jax.random.fold_in(key, 103)
    key_top = jax.random.fold_in(key, 104)
    first_block = jax.random.randint(key_first, (ABLKS,), 0, NDB // 2)
    last_block = jax.random.randint(key_last, (ABLKS,), NDB // 2, NDB)
    zero_at = jax.random.randint(key_zero, (), 0, ABLKS)
    top_at = jax.random.randint(key_top, (), 0, ABLKS)
    tile_index = jnp.arange(ABLKS, dtype=jnp.int32)
    first_block = jnp.where(tile_index == zero_at, 0, first_block)
    last_block = jnp.where(tile_index == top_at, NDB - 1, last_block)
    return (first_block.astype(jnp.int32), last_block.astype(jnp.int32), zero_at, top_at)


def draw_retina_blocks(key, part):
    first_block, last_block, zero_at, top_at = draw_pattern(key)
    return jnp.stack([first_block, last_block], axis=1).astype(jnp.int32)


def draw_quality_block(key, part):
    first_block, last_block, zero_at, top_at = draw_pattern(key)
    key_pick = jax.random.fold_in(key, 7)
    key_volume = jax.random.fold_in(key, 8)
    raw_pick = jax.random.randint(key_pick, (VOLS, ABLKS), 0, NDB)
    chosen = first_block[None, :] + raw_pick % (last_block - first_block + 1)[None, :]
    low_volume = jax.random.randint(key_volume, (), 0, VOLS)
    high_volume = (low_volume + 1) % VOLS
    volume_index = jnp.arange(VOLS, dtype=jnp.int32)[:, None]
    tile_index = jnp.arange(ABLKS, dtype=jnp.int32)[None, :]
    chosen = jnp.where((volume_index == low_volume) & (tile_index == zero_at), 0, chosen)
    chosen = jnp.where((volume_index == high_volume) & (tile_index == top_at), NDB - 1, chosen)
    return chosen.astype(jnp.int32)


def draw_quality_bias(key, part):
    return jax.random.uniform(key, (VOLS, ABLKS), jnp.float32, -2.0, 2.0)


def block_scale(rng, dims, shards, least, largest):
    level, own = 1.0, jax.random.fold_in(rng, 6)
    for position, parts in shards:
        draws = jnp.exp(jax.random.uniform(jax.random.fold_in(own, position), (parts,), jnp.float32, least / len(shards), largest / len(shards)))
        level = level * jnp.repeat(draws, dims[position] // parts).reshape([-1 if axis == position else 1 for axis in range(len(dims))])
    return level


def normal_values(own_key, shape, spread, reach, split=(), kind=jnp.bfloat16):
    values = jax.random.normal(own_key, shape, jnp.float32) * spread
    if len(split) > 0:
        values = block_scale(own_key, shape, split, -0.22, 0.18) * values
    return jnp.clip(values, min=-reach, max=reach).astype(kind)


def setup_inputs(seed: int = 0, part: int = 0) -> dict:
    streams_of = jax.random.split(jax.random.key(seed), 6)
    own_keys = jax.random.split(jax.random.fold_in(streams_of[5], part), 6)
    spectra = normal_values(own_keys[0], (VOLS, REPEATS, ALINES, K), 1.0, 6.0, ((0, 8), (2, 2)))
    block_scales = jnp.clip(jnp.exp(math.log(3.0) - 2.3025851 * jax.random.uniform(own_keys[1], (VOLS, REPEATS, ALINES, KB), jnp.float32) ** block_scale(own_keys[1], (VOLS, REPEATS, ALINES, KB), ((0, 8), (2, 2)), -0.2, 0.2)), 0.3, 3.0)
    retina_blocks = draw_retina_blocks(jax.random.fold_in(jax.random.fold_in(streams_of[5], part), 71), part)
    quality_block = draw_quality_block(jax.random.fold_in(jax.random.fold_in(streams_of[5], part), 71), part)
    quality_bias = draw_quality_bias(jax.random.fold_in(jax.random.fold_in(streams_of[5], part), 71), part)
    return {"spectra": spectra, "block_scales": block_scales, "retina_blocks": retina_blocks, "quality_block": quality_block, "quality_bias": quality_bias}


smooth_taps = (1.0 / 9.0, 2.0 / 9.0, 3.0 / 9.0, 2.0 / 9.0, 1.0 / 9.0)

def window_tables():
    sample_index = jnp.arange(K, dtype=jnp.int32)
    depth_index = jnp.arange(DEPTH, dtype=jnp.int32)
    phase_angle = (sample_index[:, None] * depth_index[None, :] % K).astype(jnp.float32) * (2.0 * math.pi / K)
    kernel = jnp.stack([jnp.cos(phase_angle), -jnp.sin(phase_angle)], axis=1)
    centres = (jnp.arange(BANDS, dtype=jnp.float32)[:, None] + 0.5) * (K / BANDS)
    distance = sample_index.astype(jnp.float32)[None, :] - centres
    offsets = distance / (K / 8.0)
    window = jnp.where(jnp.abs(distance) <= K / 2.0, jnp.exp(-0.5 * offsets * offsets), 0.0)
    window = window / jnp.sqrt(lax.optimization_barrier(jnp.sum(window * window, axis=1, keepdims=True)))
    return (window[:, :, None, None] * kernel[None]).astype(jnp.bfloat16)

def spread_columns(values, repeat_width):
    widened = jnp.broadcast_to(values[..., None], values.shape + (repeat_width,))
    return widened.reshape(values.shape[:-1] + (values.shape[-1] * repeat_width,))

def scale_spectra(spectra_vol, scales_vol):
    shaped = spectra_vol.astype(jnp.float32).reshape(scales_vol.shape + (SB,))
    return (shaped * scales_vol[..., None]).reshape(spectra_vol.shape).astype(jnp.bfloat16)

def band_maps(scaled, tables):
    line_count = scaled.shape[1]
    decorrelation = jnp.zeros((DEPTH, line_count), jnp.float32)
    power_total = jnp.zeros((DEPTH, line_count), jnp.float32)
    for band_index in range(BANDS):
        fields = jnp.einsum('kcd,rak->cdra', tables[band_index].astype(jnp.float32), scaled.astype(jnp.float32))
        band_power = fields[0] * fields[0] + fields[1] * fields[1]
        amplitude = jnp.sqrt(band_power + 0.05)
        pair_ratio = 2.0 * amplitude[:, :-1] * amplitude[:, 1:] / (band_power[:, :-1] + band_power[:, 1:] + 0.1)
        decorrelation = decorrelation + lax.optimization_barrier(jnp.sum(1.0 - pair_ratio, axis=1))
        power_total = power_total + lax.optimization_barrier(jnp.sum(band_power, axis=1))
    decorrelation = decorrelation / (BANDS * (REPEATS - 1))
    structure = jnp.log(power_total / (BANDS * REPEATS) + 0.1)
    return (decorrelation, structure)

def retina_mask(first_col, last_col):
    depth_block = jnp.arange(DEPTH, dtype=jnp.int32) // DBLK
    return (depth_block[:, None] >= first_col[None, :]) & (depth_block[:, None] <= last_col[None, :])

def lateral_smooth(padded, line_count):
    filtered = smooth_taps[0] * padded[:, 0:line_count]
    for offset_index in range(1, 5):
        filtered = filtered + smooth_taps[offset_index] * padded[:, offset_index:offset_index + line_count]
    return filtered

def block_quality(structure, qblock):
    tile_count = qblock.shape[0]
    block_means = lax.optimization_barrier(jnp.mean(structure.reshape(NDB, DBLK, tile_count, ABLK), axis=(1, 3)))
    chosen = jnp.arange(NDB, dtype=jnp.int32)[:, None] == qblock[None, :]
    return lax.optimization_barrier(jnp.sum(jnp.where(chosen, block_means, 0.0), axis=0))

def reference(spectra, block_scales, retina_blocks, quality_block, quality_bias):
    tables = window_tables()
    first_col = spread_columns(retina_blocks[:, 0], ABLK)
    last_col = spread_columns(retina_blocks[:, 1], ABLK)
    inside = retina_mask(first_col, last_col)

    def per_volume(volume_items):
        spectra_vol, scales_vol, qblock, bias_row = volume_items
        scaled = scale_spectra(spectra_vol, scales_vol)
        decorrelation, structure = band_maps(scaled, tables)
        masked_decorrelation = jnp.where(inside, decorrelation, 0.0)
        masked_structure = jnp.where(inside, structure, 0.0)
        padded = jnp.pad(masked_decorrelation, ((0, 0), (2, 2)))
        smoothed = lateral_smooth(padded, ALINES)
        volume_score = block_quality(structure, qblock) + bias_row
        return (smoothed, masked_structure, volume_score)
    smoothed, structures, scores = lax.map(per_volume, (spectra, block_scales, quality_block, quality_bias))
    weights = jnp.exp(scores - lax.optimization_barrier(jnp.max(scores, axis=0, keepdims=True)))
    weights = weights / lax.optimization_barrier(jnp.sum(weights, axis=0, keepdims=True))
    column_weights = spread_columns(weights, ABLK)[:, None, :]
    angiogram = lax.optimization_barrier(jnp.sum(column_weights * smoothed, axis=0))
    second_moment = lax.optimization_barrier(jnp.sum(column_weights * smoothed * smoothed, axis=0))
    joined_structure = lax.optimization_barrier(jnp.sum(column_weights * structures, axis=0))
    spread_map = jnp.sqrt(second_moment - angiogram * angiogram + 0.01)
    return (angiogram, joined_structure, spread_map)
```

```python
import functools
import math

import jax
import jax.numpy as jnp
import ml_dtypes
import numpy as np
from jax import lax
from jax.experimental import pallas as pl
from jax.experimental.pallas import tpu as pltpu
from jax.sharding import PartitionSpec as P

DEPTH = 512
BANDS = 4
REPEATS = 4
LANES = 128
HALO = 8
TAPS = (1.0 / 9.0, 2.0 / 9.0, 3.0 / 9.0, 2.0 / 9.0, 1.0 / 9.0)


def constants(samples):
    half = samples // 2
    distance = np.arange(half, dtype=np.float64)
    gauss = np.exp(-0.5 * (distance / (samples / 8)) ** 2)
    turn = 2.0 * np.pi * ((np.arange(half)[:, None] * np.arange(DEPTH)[None, :]) % samples) / samples
    even = gauss[:, None] * np.cos(turn)
    even[0] *= 0.5
    odd = gauss[:, None] * np.sin(turn)
    norms = []
    for band in range(BANDS):
        away = np.arange(samples) - (band + 0.5) * samples / BANDS
        window = np.where(np.abs(away) <= half, np.exp(-0.5 * (away / (samples / 8)) ** 2), 0.0)
        norms.append(float(1.0 / np.sum(window * window)))
    edge = float(np.exp(-0.5 * (half / (samples / 8)) ** 2))
    return even.astype(ml_dtypes.bfloat16), odd.astype(ml_dtypes.bfloat16), norms, edge


def maps_kernel(
    norms, edge, strips, info, bias, x_ref, scale_ref, halo_ref, even_ref, odd_ref,
    send_ref, keep_ref,
    even_in, odd_in, edge_in, power_ref, rough_ref, struct_ref,
):
    lines = LANES
    samples = x_ref.shape[-1]
    blocks = samples // LANES
    rows = REPEATS * (lines + HALO)
    lane = lax.broadcasted_iota(jnp.int32, (16, LANES), 1)
    mirror = jnp.where(lane == 0, 0, LANES - lane)
    sign = jnp.where(lane % 2 == 0, edge, -edge)

    def fold(values, row0):
        forward = [v.astype(jnp.bfloat16) for v in values]
        turned = [
            jnp.take_along_axis(v, mirror, axis=1, mode="promise_in_bounds") for v in values
        ]
        zero = jnp.zeros((16, LANES), jnp.float32)
        backward = []
        for i in range(blocks + 1):
            first = turned[blocks - i] if i > 0 else zero
            rest = turned[blocks - 1 - i] if i < blocks else zero
            backward.append(jnp.where(lane == 0, first, rest).astype(jnp.bfloat16))
        span = blocks // BANDS
        for band in range(BANDS):
            centre = span // 2 + span * band
            for i in range(blocks // 2):
                ahead = forward[centre + i] if centre + i < blocks else None
                j = blocks - centre + i
                behind = backward[j] if j <= blocks else None
                if behind is None:
                    plus, minus = ahead, ahead
                elif ahead is None:
                    plus, minus = behind, -behind
                else:
                    plus, minus = ahead + behind, ahead - behind
                at = (band, pl.ds(row0, 16), pl.ds(i * LANES, LANES))
                even_in[at] = plus
                odd_in[at] = minus
            far = centre + blocks // 2
            far = far if far < blocks else centre - blocks // 2
            value = forward[far].astype(jnp.float32)[:, :1]
            edge_in[band, pl.ds(row0, 16), :] = value * sign

    per = lines // 16

    def fold_group(g, carry):
        r, line0 = g // per, pl.multiple_of((g % per) * 16, 16)
        values = []
        for kb in range(blocks):
            v = x_ref[r, pl.ds(line0, 16), pl.ds(kb * LANES, LANES)].astype(jnp.float32)
            values.append(v * scale_ref[r, pl.ds(line0, 16), kb : kb + 1])
        fold(values, pl.multiple_of(g * 16, 16))
        return carry

    lax.fori_loop(0, REPEATS * per, fold_group, 0, unroll=2)
    for h in range(REPEATS * HALO // 16):
        fold(
            [halo_ref[h * 16 : h * 16 + 16, kb * LANES : (kb + 1) * LANES] for kb in range(blocks)],
            REPEATS * lines + h * 16,
        )

    for band in range(BANDS):
        re = jnp.dot(even_in[band], even_ref[...], preferred_element_type=jnp.float32)
        im = jnp.dot(odd_in[band], odd_ref[...], preferred_element_type=jnp.float32)
        extra = edge_in[band]
        extra = jnp.concatenate([extra] * (DEPTH // LANES), axis=1)
        re = re + extra
        power_ref[band] = re * re + im * im + 0.05 / norms[band]

    def finish(starts):
        ratio, total = None, None
        for band in range(BANDS):
            powers = [power_ref[band, pl.ds(s, 8), :] for s in starts]
            level = (powers[0] + powers[1]) + (powers[2] + powers[3])
            level = level * (norms[band] / (BANDS * REPEATS))
            total = level if total is None else total + level
            for p, q in zip(powers[:-1], powers[1:]):
                product, both = p * q, p + q
                part = product * lax.rsqrt(product * (both * both))
                ratio = part if ratio is None else ratio + part
        rough = 1.0 - ratio * (2.0 / (BANDS * (REPEATS - 1)))
        return rough, jnp.log(total + 0.05)

    def shut(values, first, last):
        out = []
        for zb in range(DEPTH // LANES):
            inside = jnp.logical_and(first <= zb, zb <= last)
            out.append(jnp.where(inside, values[:, zb * LANES : (zb + 1) * LANES], 0.0))
        return jnp.concatenate(out, axis=1)

    first, last = info[3], info[4]

    def finish_group(g, carry):
        line0 = pl.multiple_of(g * 8, 8)
        rough, struct = finish([r * lines + line0 for r in range(REPEATS)])
        rough_ref[pl.ds(line0 + 8, 8), :] = shut(rough, first, last)
        struct_ref[pl.ds(line0, 8), :] = struct
        return carry

    lax.fori_loop(0, lines // 8, finish_group, 0)
    rough, _ = finish([REPEATS * lines + r * HALO for r in range(REPEATS)])
    rough_ref[6:8, :] = shut(rough[0:2], info[1], info[2])
    rough_ref[8 + lines : 10 + lines, :] = shut(rough[2:4], info[5], info[6])

    chosen = struct_ref[:, pl.ds(pl.multiple_of(info[7] * LANES, LANES), LANES)]
    score = jnp.sum(chosen) * (1.0 / (LANES * lines)) + bias[0]
    smooth = TAPS[0] * rough_ref[6 : 6 + lines, :]
    for k in range(1, 5):
        smooth = smooth + TAPS[k] * rough_ref[6 + k : 6 + k + lines, :]
    maps = (smooth, shut(struct_ref[...], first, last))
    half = (send_ref.shape[0] - 8) // 2
    strip = DEPTH // strips
    low = info[8] == 0
    for m, whole in enumerate(maps):
        for zb in range(DEPTH // LANES):
            block = whole[:, zb * LANES : (zb + 1) * LANES].T
            for s in range(LANES // (2 * strip)):
                a = block[2 * s * strip : (2 * s + 1) * strip]
                b = block[(2 * s + 1) * strip : (2 * s + 2) * strip]
                at = m * half + zb * (LANES // 2) + s * strip
                keep_ref[at : at + strip, :] = jnp.where(low, a, b)
                send_ref[at : at + strip, :] = jnp.where(low, b, a)
    row = jnp.full((8, lines), score, jnp.float32)
    keep_ref[2 * half :, :] = row
    send_ref[2 * half :, :] = row


def maps_call(info, bias, spectra, scales, halo, even, odd, norms, edge, strips):
    samples = spectra.shape[-1]
    rows = REPEATS * (LANES + HALO)
    out = jax.ShapeDtypeStruct((DEPTH + 8, LANES), jnp.float32)
    half = samples // 2
    return pl.pallas_call(
        functools.partial(maps_kernel, norms, edge, strips),
        grid_spec=pltpu.PrefetchScalarGridSpec(
            num_scalar_prefetch=2,
            grid=(1,),
            in_specs=[
                pl.BlockSpec((REPEATS, LANES, samples), lambda i, info, bias: (0, info[0], 0)),
                pl.BlockSpec((REPEATS, LANES, samples // LANES), lambda i, info, bias: (0, info[0], 0)),
                pl.BlockSpec((REPEATS * HALO, samples), lambda i, info, bias: (0, 0)),
                pl.BlockSpec((half, DEPTH), lambda i, info, bias: (0, 0)),
                pl.BlockSpec((half, DEPTH), lambda i, info, bias: (0, 0)),
            ],
            out_specs=[pl.BlockSpec((DEPTH + 8, LANES), lambda i, info, bias: (0, 0))] * 2,
            scratch_shapes=[
                pltpu.VMEM((BANDS, rows, half), jnp.bfloat16),
                pltpu.VMEM((BANDS, rows, half), jnp.bfloat16),
                pltpu.VMEM((BANDS, rows, LANES), jnp.float32),
                pltpu.VMEM((BANDS, rows, DEPTH), jnp.float32),
                pltpu.VMEM((LANES + 16, DEPTH), jnp.float32),
                pltpu.VMEM((LANES, DEPTH), jnp.float32),
            ],
        ),
        out_shape=[out, out],
        compiler_params=pltpu.CompilerParams(vmem_limit_bytes=48 * 1024 * 1024),
        name="maps",
    )(info, bias, spectra, scales, halo, even, odd)


def part_rows(half):
    return 3 * half + 16


def merged(stage_raw, keep_ref, recv_ref, rows):
    if stage_raw:
        half = rows
        top_a, top_b = keep_ref[2 * half : 2 * half + 1], recv_ref[2 * half : 2 * half + 1]
        top = jnp.maximum(top_a, top_b)
        wa, wb = jnp.exp(top_a - top), jnp.exp(top_b - top)
        sa, sb = keep_ref[:half], recv_ref[:half]
        first = wa * sa
        other = wb * sb
        maps = [
            first + other,
            first * sa + other * sb,
            wa * keep_ref[half : 2 * half] + wb * recv_ref[half : 2 * half],
        ]
        return maps, top, wa + wb
    at = 3 * rows
    top_a, top_b = keep_ref[at : at + 1], recv_ref[at : at + 1]
    top = jnp.maximum(top_a, top_b)
    wa, wb = jnp.exp(top_a - top), jnp.exp(top_b - top)
    maps = [
        wa * keep_ref[m * rows : (m + 1) * rows] + wb * recv_ref[m * rows : (m + 1) * rows]
        for m in range(3)
    ]
    return maps, top, wa * keep_ref[at + 8 : at + 9] + wb * recv_ref[at + 8 : at + 9]


def merge_kernel(stage_raw, rows, strip, bit, keep_ref, recv_ref, send_out, keep_out):
    maps, top, weight = merged(stage_raw, keep_ref, recv_ref, rows)
    low = bit[0] == 0
    half = rows // 2
    for m, whole in enumerate(maps):
        for s in range(half // strip):
            a = whole[2 * s * strip : (2 * s + 1) * strip]
            b = whole[(2 * s + 1) * strip : (2 * s + 2) * strip]
            at = m * half + s * strip
            keep_out[at : at + strip] = jnp.where(low, a, b)
            send_out[at : at + strip] = jnp.where(low, b, a)
    tail = 3 * half
    for out in (keep_out, send_out):
        out[tail : tail + 8] = jnp.broadcast_to(top, (8, LANES))
        out[tail + 8 : tail + 16] = jnp.broadcast_to(weight, (8, LANES))


def merge_call(bit, keep, recv, rows, strip, stage_raw):
    out = jax.ShapeDtypeStruct((part_rows(rows // 2), LANES), jnp.float32)
    whole = pl.BlockSpec(memory_space=pltpu.VMEM)
    return pl.pallas_call(
        functools.partial(merge_kernel, stage_raw, rows, strip),
        in_specs=[pl.BlockSpec(memory_space=pltpu.SMEM), whole, whole],
        out_specs=[whole, whole],
        out_shape=[out, out],
        name="merge",
    )(bit, keep, recv)


def final_kernel(stage_raw, rows, count, order, *refs):
    keeps, recvs = refs[:count], refs[count : 2 * count]
    angio_ref, joined_ref, spread_ref = refs[2 * count :]
    for i in range(count):
        maps, _, weight = merged(stage_raw, keeps[i], recvs[i], rows)
        scale = 1.0 / weight
        mean = maps[0] * scale
        columns = pl.ds(pl.multiple_of(order[i] * LANES, LANES), LANES)
        angio_ref[:, columns] = mean
        joined_ref[:, columns] = maps[2] * scale
        spread_ref[:, columns] = jnp.sqrt(maps[1] * scale - mean * mean + 0.01)


def final_call(order, keeps, recvs, rows, stage_raw):
    count = len(keeps)
    whole = pl.BlockSpec(memory_space=pltpu.VMEM)
    out = jax.ShapeDtypeStruct((rows, count * LANES), jnp.float32)
    return pl.pallas_call(
        functools.partial(final_kernel, stage_raw, rows, count),
        in_specs=[pl.BlockSpec(memory_space=pltpu.SMEM)] + [whole] * (2 * count),
        out_specs=[whole] * 3,
        out_shape=[out] * 3,
        name="final",
    )(order, *keeps, *recvs)


def scaled_lines(spectra, scales, start):
    lines = lax.dynamic_slice_in_dim(spectra, start, 2, axis=1).astype(jnp.float32)
    level = lax.dynamic_slice_in_dim(scales, start, 2, axis=1)
    shaped = lines.reshape(level.shape + (-1,)) * level[..., None]
    return shaped.reshape(lines.shape)


def on_device(tiles, strips, spectra, scales, retina, quality, bias):
    spectra, scales, quality, bias = spectra[0], scales[0], quality[0], bias[0]
    samples = spectra.shape[-1]
    count = retina.shape[0]
    even, odd, norms, edge = constants(samples)
    even, odd = jnp.asarray(even), jnp.asarray(odd)
    here = lax.axis_index("tile")
    vol = lax.axis_index("vol")
    lines = spectra.shape[1]
    none = jnp.array([1 << 20, -1], jnp.int32)

    def packed(start, block):
        rows = scaled_lines(spectra, scales, start).reshape(-1, samples)
        extra = jnp.broadcast_to(block.astype(jnp.float32)[:, None], (2, samples))
        return jnp.concatenate([rows, extra], axis=0)

    def unpacked(array):
        block = array[-2:, 0].astype(jnp.int32)
        return array[:-2].reshape(REPEATS, 2, samples), block

    if tiles == 2:
        flip = here == 1
        start = jnp.where(flip, 0, lines - 2)
        own = packed(start, jnp.where(flip, retina[0], retina[count - 1]))
        ahead, block = unpacked(lax.ppermute(own, "tile", [(0, 1), (1, 0)]))
        before, before_block, after, after_block = ahead, block, ahead, block
        outside = [(False, False)] * (count - 1) + [(True, True)]
    else:
        flip = here < 0
        up = [(i, i + 1) for i in range(tiles - 1)]
        down = [(i + 1, i) for i in range(tiles - 1)]
        before, before_block = unpacked(
            lax.ppermute(packed(lines - 2, retina[count - 1]), "tile", up)
        )
        after, after_block = unpacked(lax.ppermute(packed(0, retina[0]), "tile", down))
        outside = [(i == 0, i == count - 1) for i in range(count)]
    before_block = jnp.where(here == 0, none, before_block)
    after_block = jnp.where(here == tiles - 1, none, after_block)

    bits = strips.bit_length() - 1
    order, keeps, sends = [], [], []
    for i in range(count):
        t = jnp.where(flip, count - 1 - i, i)
        order.append(t)
        prev_line = jnp.maximum(t * LANES - 2, 0)
        next_line = jnp.minimum(t * LANES + LANES, lines - 2)
        prev = scaled_lines(spectra, scales, prev_line)
        nxt = scaled_lines(spectra, scales, next_line)
        prev_block = lax.dynamic_index_in_dim(retina, jnp.maximum(t - 1, 0), 0, False)
        next_block = lax.dynamic_index_in_dim(retina, jnp.minimum(t + 1, count - 1), 0, False)
        if outside[i][0]:
            prev = jnp.where(t == 0, before, prev)
            prev_block = jnp.where(t == 0, before_block, prev_block)
        else:
            prev_block = jnp.where(t == 0, none, prev_block)
        if outside[i][1]:
            nxt = jnp.where(t == count - 1, after, nxt)
            next_block = jnp.where(t == count - 1, after_block, next_block)
        else:
            next_block = jnp.where(t == count - 1, none, next_block)
        halo = jnp.concatenate([prev, nxt, jnp.zeros((REPEATS, HALO - 4, samples), jnp.float32)], axis=1)
        block = lax.dynamic_index_in_dim(retina, t, 0, False)
        pick = lax.dynamic_index_in_dim(quality, t, 0)
        info = jnp.concatenate(
            [t[None], prev_block, block, next_block, pick, (vol & 1)[None]]
        ).astype(jnp.int32)
        send, keep = maps_call(
            info, lax.dynamic_index_in_dim(bias, t, 0), spectra, scales,
            halo.reshape(REPEATS * HALO, samples), even, odd, norms, edge, strips,
        )
        keeps.append(keep)
        sends.append(send)

    strip = DEPTH // strips
    rows = DEPTH // 2
    for stage in range(bits):
        pairs = [(v, v ^ (1 << stage)) for v in range(strips)]
        recvs = [lax.ppermute(s, "vol", pairs) for s in sends]
        if stage == bits - 1:
            return tuple(final_call(jnp.stack(order), keeps, recvs, rows, stage == 0))
        bit = ((vol >> (stage + 1)) & 1)[None]
        both = [
            merge_call(bit, k, r, rows, strip, stage == 0) for k, r in zip(keeps, recvs)
        ]
        sends, keeps = [b[0] for b in both], [b[1] for b in both]
        rows //= 2


def solution(mesh):
    return jax.shard_map(
        functools.partial(on_device, mesh.shape["tile"], mesh.shape["vol"]),
        mesh=mesh,
        in_specs=(
            P(("study", "vol"), None, "tile", None),
            P(("study", "vol"), None, "tile", None),
            P(("study", "tile"), None),
            P(("study", "vol"), "tile"),
            P(("study", "vol"), "tile"),
        ),
        out_specs=(P(("study", "vol"), "tile"),) * 3,
        check_vma=False,
    )
```

```python
import functools
import math

import jax
import jax.numpy as jnp
import ml_dtypes
import numpy as np
from jax import lax
from jax.experimental import pallas as pl
from jax.experimental.pallas import tpu as pltpu
from jax.sharding import PartitionSpec as P

DEPTH = 512
BANDS = 4
REPEATS = 4
LANES = 128
HALO = 8
TAPS = (1.0 / 9.0, 2.0 / 9.0, 3.0 / 9.0, 2.0 / 9.0, 1.0 / 9.0)


def constants(samples):
    half = samples // 2
    distance = np.arange(half, dtype=np.float64)
    gauss = np.exp(-0.5 * (distance / (samples / 8)) ** 2)
    turn = 2.0 * np.pi * ((np.arange(half)[:, None] * np.arange(DEPTH)[None, :]) % samples) / samples
    even = gauss[:, None] * np.cos(turn)
    even[0] *= 0.5
    odd = gauss[:, None] * np.sin(turn)
    norms = []
    for band in range(BANDS):
        away = np.arange(samples) - (band + 0.5) * samples / BANDS
        window = np.where(np.abs(away) <= half, np.exp(-0.5 * (away / (samples / 8)) ** 2), 0.0)
        norms.append(float(1.0 / np.sum(window * window)))
    edge = float(np.exp(-0.5 * (half / (samples / 8)) ** 2))
    return even.astype(ml_dtypes.bfloat16), odd.astype(ml_dtypes.bfloat16), norms, edge


def maps_kernel(
    norms, edge, strips, step, count, outer, info, bias, x_hbm, scale_ref, ext_ref, even_hbm, odd_hbm,
    send_ref, keep_ref,
    rough_ref, struct_ref, x_ref, level_ref, near_ref, even_ref, odd_ref, sems, *scratch,
):
    lines = LANES
    samples = x_hbm.shape[-1]
    blocks = samples // LANES
    parts = lines // SUB
    rows = REPEATS * SUB
    flip = info[0]
    tile = jnp.where(flip == 1, count - 1 - step, step)
    lane = lax.broadcasted_iota(jnp.int32, (SUB, LANES), 1)
    mirror = jnp.where(lane == 0, 0, LANES - lane)
    sign = jnp.where(lane % 2 == 0, edge, -edge)

    line_count = x_hbm.shape[1]
    base = pl.multiple_of(tile * lines, lines)
    base_prev = pl.multiple_of(jnp.maximum(base - SUB, 0), SUB)
    base_next = pl.multiple_of(jnp.minimum(base + lines, line_count - SUB), SUB)
    own = pltpu.make_async_copy(
        x_hbm.at[:, pl.ds(base, lines), :], x_ref.at[:, :lines, :], sems.at[0]
    )
    tables = [
        pltpu.make_async_copy(even_hbm, even_ref, sems.at[1]),
        pltpu.make_async_copy(odd_hbm, odd_ref, sems.at[2]),
    ]
    edges = [
        pltpu.make_async_copy(x_hbm.at[:, pl.ds(start, SUB), :], near_ref.at[n], sems.at[3 + n])
        for n, start in enumerate((base_prev, base_next))
    ]
    for copy in [own] + edges + tables:
        copy.start()

    at_start, at_end = tile == 0, tile == count - 1
    whole_prev = pl.ds(pl.multiple_of(jnp.maximum(base - lines, 0), lines), lines)
    whole_next = pl.ds(pl.multiple_of(jnp.minimum(base + lines, line_count - lines), lines), lines)

    def placed(values, at):
        above = jnp.zeros((at, values.shape[1]), values.dtype)
        below = jnp.zeros((SUB - 2 - at, values.shape[1]), values.dtype)
        return jnp.concatenate([piece for piece in (above, values, below) if piece.shape[0]], axis=0)

    row_of = lax.broadcasted_iota(jnp.int32, (SUB, blocks), 0)
    for r in range(REPEATS):
        level_ref[r, :lines, :] = scale_ref[r, :, pl.ds(base, lines)].T
        level_prev = scale_ref[r, :, whole_prev].T[lines - SUB :]
        level_next = scale_ref[r, :, whole_next].T[:SUB]
        outside = ext_ref[2 * r : 2 * r + 2, samples : samples + blocks]
        if outer[0]:
            level_prev = jnp.where(at_start, placed(outside, SUB - 2), level_prev)
        if outer[1]:
            level_next = jnp.where(at_end, placed(outside, 0), level_next)
        level_ref[r, lines:, :] = jnp.where(row_of < 2, level_next, level_prev)

    for copy in [own] + edges:
        copy.wait()
    for r in range(REPEATS):
        for kb in range(blocks):
            columns = slice(kb * LANES, (kb + 1) * LANES)
            a = near_ref[0, r, :, columns].astype(jnp.float32)
            b = near_ref[1, r, :, columns].astype(jnp.float32)
            if outer[0]:
                a = jnp.where(at_start, placed(ext_ref[2 * r : 2 * r + 2, columns], SUB - 2), a)
            if outer[1]:
                b = jnp.where(at_end, placed(ext_ref[2 * r : 2 * r + 2, columns], 0), b)
            low = lax.broadcasted_iota(jnp.int32, (SUB, LANES), 0) < 2
            x_ref[r, lines:, columns] = jnp.where(low, b, a).astype(jnp.bfloat16)

    def fold(s, buffers):
        even_in, odd_in, edge_in = buffers
        for r in range(REPEATS):
            at = pl.ds(pl.multiple_of(s * SUB, SUB), SUB)
            level = level_ref[r, at, :]
            values = [
                x_ref[r, at, kb * LANES : (kb + 1) * LANES].astype(jnp.float32)
                * level[:, kb : kb + 1]
                for kb in range(blocks)
            ]
            forward = [v.astype(jnp.bfloat16) for v in values]
            turned = [
                jnp.take_along_axis(v, mirror, axis=1, mode="promise_in_bounds") for v in values
            ]
            zero = jnp.zeros((SUB, LANES), jnp.float32)
            backward = []
            for i in range(blocks + 1):
                first = turned[blocks - i] if i > 0 else zero
                rest = turned[blocks - 1 - i] if i < blocks else zero
                backward.append(jnp.where(lane == 0, first, rest).astype(jnp.bfloat16))
            span = blocks // BANDS
            for band in range(BANDS):
                to = slice(band * rows + r * SUB, band * rows + r * SUB + SUB)
                centre = span // 2 + span * band
                for i in range(blocks // 2):
                    ahead = forward[centre + i] if centre + i < blocks else None
                    j = blocks - centre + i
                    behind = backward[j] if j <= blocks else None
                    if behind is None:
                        plus, minus = ahead, ahead
                    elif ahead is None:
                        plus, minus = behind, -behind
                    else:
                        plus, minus = ahead + behind, ahead - behind
                    even_in[to, i * LANES : (i + 1) * LANES] = plus
                    odd_in[to, i * LANES : (i + 1) * LANES] = minus
                far = centre + blocks // 2
                far = far if far < blocks else centre - blocks // 2
                edge_in[to, :] = forward[far].astype(jnp.float32)[:, :1] * sign

    def limits(t):
        return info[2 + 2 * t], info[3 + 2 * t]

    first, last = limits(tile)
    prev_first, prev_last = limits(jnp.maximum(tile - 1, 0))
    next_first, next_last = limits(jnp.minimum(tile + 1, count - 1))
    out_at = 2 + 3 * count
    prev_first = jnp.where(at_start, info[out_at] if outer[0] else 1 << 20, prev_first)
    prev_last = jnp.where(at_start, info[out_at + 1] if outer[0] else -1, prev_last)
    next_first = jnp.where(at_end, info[out_at + 2] if outer[1] else 1 << 20, next_first)
    next_last = jnp.where(at_end, info[out_at + 3] if outer[1] else -1, next_last)

    def shut(values, low, high, at=0):
        out = []
        for n in range(values.shape[1] // LANES):
            inside = jnp.logical_and(low <= at + n, at + n <= high)
            out.append(jnp.where(inside, values[:, n * LANES : (n + 1) * LANES], 0.0))
        return jnp.concatenate(out, axis=1)

    def finish(powers_of):
        ratio, total = None, None
        for band in range(BANDS):
            powers = [powers_of(band, r) for r in range(REPEATS)]
            level = (powers[0] + powers[1]) + (powers[2] + powers[3])
            level = level * (norms[band] / (BANDS * REPEATS))
            total = level if total is None else total + level
            for p, q in zip(powers[:-1], powers[1:]):
                product, both = p * q, p + q
                part = product * lax.rsqrt(product * (both * both))
                ratio = part if ratio is None else ratio + part
        rough = 1.0 - ratio * (2.0 / (BANDS * (REPEATS - 1)))
        return rough, jnp.log(total + 0.05)

    def dots(s, buffers, border):
        even_in, odd_in, edge_in = buffers
        wide = DEPTH // SPLIT
        for part in range(SPLIT):
            columns = slice(part * wide, (part + 1) * wide)
            re = jnp.dot(even_in[...], even_ref[:, columns], preferred_element_type=jnp.float32)
            im = jnp.dot(odd_in[...], odd_ref[:, columns], preferred_element_type=jnp.float32)
            block0 = part * (wide // LANES)
            for g in range(SUB // 8):

                def power(band, r):
                    at = slice(band * rows + r * SUB + g * 8, band * rows + r * SUB + g * 8 + 8)
                    extra = jnp.concatenate([edge_in[at]] * (wide // LANES), axis=1)
                    a, b = re[at] + extra, im[at]
                    return a * a + b * b + 0.05 / norms[band]

                rough, struct = finish(power)
                if border:
                    rough_ref[g * 8 : g * 8 + 8, columns] = shut(rough, prev_first, prev_last, block0)
                    at = SUB + lines + g * 8
                    rough_ref[at : at + 8, columns] = shut(rough, next_first, next_last, block0)
                else:
                    line0 = pl.multiple_of(s * SUB + g * 8, 8)
                    rough_ref[pl.ds(line0 + SUB, 8), columns] = shut(rough, first, last, block0)
                    struct_ref[pl.ds(line0, 8), columns] = struct

    bufs = [scratch[0:3], scratch[3:6]]
    fold(0, bufs[0])
    for copy in tables:
        copy.wait()

    def pair(i, carry):
        dots(2 * i, bufs[0], False)
        fold(2 * i + 1, bufs[1])
        dots(2 * i + 1, bufs[1], False)
        fold(2 * i + 2, bufs[0])
        return carry

    lax.fori_loop(0, parts // 2, pair, 0)
    dots(parts, bufs[0], True)

    pick = info[2 + 2 * count + tile]
    chosen = struct_ref[:, pl.ds(pl.multiple_of(pick * LANES, LANES), LANES)]
    score = jnp.sum(chosen) * (1.0 / (LANES * lines)) + bias[tile]
    smooth = TAPS[0] * rough_ref[SUB - 2 : SUB - 2 + lines, :]
    for k in range(1, 5):
        smooth = smooth + TAPS[k] * rough_ref[SUB - 2 + k : SUB - 2 + k + lines, :]
    maps = (smooth, shut(struct_ref[...], first, last))
    half = (send_ref.shape[0] - 8) // 2
    strip = DEPTH // strips
    low = info[1] % 2 == 0
    for m, whole in enumerate(maps):
        for zb in range(DEPTH // LANES):
            block = whole[:, zb * LANES : (zb + 1) * LANES].T
            for s in range(LANES // (2 * strip)):
                a = block[2 * s * strip : (2 * s + 1) * strip]
                b = block[(2 * s + 1) * strip : (2 * s + 2) * strip]
                at = m * half + zb * (LANES // 2) + s * strip
                keep_ref[at : at + strip, :] = jnp.where(low, a, b)
                send_ref[at : at + strip, :] = jnp.where(low, b, a)
    row = jnp.full((8, lines), score, jnp.float32)
    keep_ref[2 * half :, :] = row
    send_ref[2 * half :, :] = row


SUB = 16
SPLIT = 2


def maps_call(step, count, outer, info, bias, spectra, scales, ext, even, odd, norms, edge, strips):
    samples = spectra.shape[-1]
    rows = BANDS * REPEATS * SUB
    out = jax.ShapeDtypeStruct((DEPTH + 8, LANES), jnp.float32)
    half = samples // 2
    whole = pl.BlockSpec(memory_space=pltpu.VMEM)
    remote = pl.BlockSpec(memory_space=pl.ANY)
    pair = [
        pltpu.VMEM((rows, half), jnp.bfloat16),
        pltpu.VMEM((rows, half), jnp.bfloat16),
        pltpu.VMEM((rows, LANES), jnp.float32),
    ]
    return pl.pallas_call(
        functools.partial(maps_kernel, norms, edge, strips, step, count, outer),
        in_specs=[pl.BlockSpec(memory_space=pltpu.SMEM)] * 2 + [remote, whole, whole, remote, remote],
        out_specs=[whole] * 2,
        scratch_shapes=[
            pltpu.VMEM((LANES + 2 * SUB, DEPTH), jnp.float32),
            pltpu.VMEM((LANES, DEPTH), jnp.float32),
            pltpu.VMEM((REPEATS, LANES + SUB, samples), jnp.bfloat16),
            pltpu.VMEM((REPEATS, LANES + SUB, samples // LANES), jnp.float32),
            pltpu.VMEM((2, REPEATS, SUB, samples), jnp.bfloat16),
            pltpu.VMEM((half, DEPTH), jnp.bfloat16),
            pltpu.VMEM((half, DEPTH), jnp.bfloat16),
            pltpu.SemaphoreType.DMA((5,)),
        ] + pair + pair,
        out_shape=[out, out],
        compiler_params=pltpu.CompilerParams(vmem_limit_bytes=48 * 1024 * 1024),
        name="maps",
    )(info, bias, spectra, jnp.swapaxes(scales, 1, 2), ext, even, odd)


def part_rows(half):
    return 3 * half + 16


def merged(stage_raw, keep_ref, recv_ref, rows):
    if stage_raw:
        half = rows
        top_a, top_b = keep_ref[2 * half : 2 * half + 1], recv_ref[2 * half : 2 * half + 1]
        top = jnp.maximum(top_a, top_b)
        wa, wb = jnp.exp(top_a - top), jnp.exp(top_b - top)
        sa, sb = keep_ref[:half], recv_ref[:half]
        first = wa * sa
        other = wb * sb
        maps = [
            first + other,
            first * sa + other * sb,
            wa * keep_ref[half : 2 * half] + wb * recv_ref[half : 2 * half],
        ]
        return maps, top, wa + wb
    at = 3 * rows
    top_a, top_b = keep_ref[at : at + 1], recv_ref[at : at + 1]
    top = jnp.maximum(top_a, top_b)
    wa, wb = jnp.exp(top_a - top), jnp.exp(top_b - top)
    maps = [
        wa * keep_ref[m * rows : (m + 1) * rows] + wb * recv_ref[m * rows : (m + 1) * rows]
        for m in range(3)
    ]
    return maps, top, wa * keep_ref[at + 8 : at + 9] + wb * recv_ref[at + 8 : at + 9]


def merge_kernel(stage_raw, rows, strip, bit, keep_ref, recv_ref, send_out, keep_out):
    maps, top, weight = merged(stage_raw, keep_ref, recv_ref, rows)
    low = bit[0] == 0
    half = rows // 2
    for m, whole in enumerate(maps):
        for s in range(half // strip):
            a = whole[2 * s * strip : (2 * s + 1) * strip]
            b = whole[(2 * s + 1) * strip : (2 * s + 2) * strip]
            at = m * half + s * strip
            keep_out[at : at + strip] = jnp.where(low, a, b)
            send_out[at : at + strip] = jnp.where(low, b, a)
    tail = 3 * half
    for out in (keep_out, send_out):
        out[tail : tail + 8] = jnp.broadcast_to(top, (8, LANES))
        out[tail + 8 : tail + 16] = jnp.broadcast_to(weight, (8, LANES))


def merge_call(bit, keep, recv, rows, strip, stage_raw):
    out = jax.ShapeDtypeStruct((part_rows(rows // 2), LANES), jnp.float32)
    whole = pl.BlockSpec(memory_space=pltpu.VMEM)
    return pl.pallas_call(
        functools.partial(merge_kernel, stage_raw, rows, strip),
        in_specs=[pl.BlockSpec(memory_space=pltpu.SMEM), whole, whole],
        out_specs=[whole, whole],
        out_shape=[out, out],
        name="merge",
    )(bit, keep, recv)


def final_kernel(stage_raw, rows, count, order, *refs):
    keeps, recvs = refs[:count], refs[count : 2 * count]
    angio_ref, joined_ref, spread_ref = refs[2 * count :]
    for i in range(count):
        maps, _, weight = merged(stage_raw, keeps[i], recvs[i], rows)
        scale = 1.0 / weight
        mean = maps[0] * scale
        columns = pl.ds(pl.multiple_of(order[i] * LANES, LANES), LANES)
        angio_ref[:, columns] = mean
        joined_ref[:, columns] = maps[2] * scale
        spread_ref[:, columns] = jnp.sqrt(maps[1] * scale - mean * mean + 0.01)


def final_call(order, keeps, recvs, rows, stage_raw):
    count = len(keeps)
    whole = pl.BlockSpec(memory_space=pltpu.VMEM)
    out = jax.ShapeDtypeStruct((rows, count * LANES), jnp.float32)
    return pl.pallas_call(
        functools.partial(final_kernel, stage_raw, rows, count),
        in_specs=[pl.BlockSpec(memory_space=pltpu.SMEM)] + [whole] * (2 * count),
        out_specs=[whole] * 3,
        out_shape=[out] * 3,
        name="final",
    )(order, *keeps, *recvs)


def edge_rows(spectra, scales, start, block):
    lines = lax.dynamic_slice_in_dim(spectra, start, 2, axis=1).astype(jnp.float32)
    level = lax.dynamic_slice_in_dim(scales, start, 2, axis=1)
    rows = lines.shape[0] * 2
    limits = jnp.broadcast_to(block.astype(jnp.float32)[None], (rows, 2))
    rest = jnp.zeros((rows, LANES - level.shape[2] - 2), jnp.float32)
    return jnp.concatenate(
        [lines.reshape(rows, -1), level.reshape(rows, -1), limits, rest], axis=1
    )


def on_device(tiles, strips, spectra, scales, retina, quality, bias):
    spectra, scales, quality, bias = spectra[0], scales[0], quality[0], bias[0]
    samples = spectra.shape[-1]
    count = retina.shape[0]
    even, odd, norms, edge = constants(samples)
    even, odd = jnp.asarray(even), jnp.asarray(odd)
    here = lax.axis_index("tile")
    vol = lax.axis_index("vol")
    lines = spectra.shape[1]

    if tiles == 2:
        flip = (here == 1).astype(jnp.int32)
        start = jnp.where(here == 1, 0, lines - 2)
        own = edge_rows(spectra, scales, start, jnp.where(here == 1, retina[0], retina[count - 1]))
        before = after = lax.ppermute(own, "tile", [(0, 1), (1, 0)])
        outside = [(False, False)] * (count - 1) + [(True, True)]
    else:
        flip = jnp.zeros((), jnp.int32)
        up = [(i, i + 1) for i in range(tiles - 1)]
        down = [(i + 1, i) for i in range(tiles - 1)]
        before = lax.ppermute(edge_rows(spectra, scales, lines - 2, retina[count - 1]), "tile", up)
        after = lax.ppermute(edge_rows(spectra, scales, 0, retina[0]), "tile", down)
        outside = [(i == 0, i == count - 1) for i in range(count)]
    info = jnp.concatenate([flip[None], vol[None], retina.reshape(-1), quality]).astype(jnp.int32)
    none = jnp.array([1 << 20, -1], jnp.int32)
    at = samples + scales.shape[2]
    before_block = jnp.where(here == 0, none, before[0, at : at + 2].astype(jnp.int32))
    after_block = jnp.where(here == tiles - 1, none, after[0, at : at + 2].astype(jnp.int32))
    info_outer = jnp.concatenate([info, before_block, after_block])

    bits = strips.bit_length() - 1
    order, keeps, sends = [], [], []
    for i in range(count):
        order.append(jnp.where(flip == 1, count - 1 - i, i))
        outer = outside[i]
        ext = after if outer[1] else (before if outer[0] else jnp.zeros((2 * REPEATS, samples + LANES), jnp.float32))
        if tiles != 2 and outer[0] and outer[1]:
            raise ValueError("one tile")
        send, keep = maps_call(
            i, count, outer, info_outer if outer[0] or outer[1] else info, bias,
            spectra, scales, ext, even, odd, norms, edge, strips,
        )
        keeps.append(keep)
        sends.append(send)

    strip = DEPTH // strips
    rows = DEPTH // 2
    for stage in range(bits):
        pairs = [(v, v ^ (1 << stage)) for v in range(strips)]
        recvs = [lax.ppermute(s, "vol", pairs) for s in sends]
        if stage == bits - 1:
            return tuple(final_call(jnp.stack(order), keeps, recvs, rows, stage == 0))
        bit = ((vol >> (stage + 1)) & 1)[None]
        both = [
            merge_call(bit, k, r, rows, strip, stage == 0) for k, r in zip(keeps, recvs)
        ]
        sends, keeps = [b[0] for b in both], [b[1] for b in both]
        rows //= 2


def solution(mesh):
    return jax.shard_map(
        functools.partial(on_device, mesh.shape["tile"], mesh.shape["vol"]),
        mesh=mesh,
        in_specs=(
            P(("study", "vol"), None, "tile", None),
            P(("study", "vol"), None, "tile", None),
            P(("study", "tile"), None),
            P(("study", "vol"), "tile"),
            P(("study", "vol"), "tile"),
        ),
        out_specs=(P(("study", "vol"), "tile"),) * 3,
        check_vma=False,
    )
```

```python
import functools
import math

import jax
import jax.numpy as jnp
import ml_dtypes
import numpy as np
from jax import lax
from jax.experimental import pallas as pl
from jax.experimental.pallas import tpu as pltpu
from jax.sharding import PartitionSpec as P

DEPTH = 512
BANDS = 4
REPEATS = 4
LANES = 128
HALO = 8
TAPS = (1.0 / 9.0, 2.0 / 9.0, 3.0 / 9.0, 2.0 / 9.0, 1.0 / 9.0)


def constants(samples):
    half = samples // 2
    distance = np.arange(half, dtype=np.float64)
    gauss = np.exp(-0.5 * (distance / (samples / 8)) ** 2)
    turn = 2.0 * np.pi * ((np.arange(half)[:, None] * np.arange(DEPTH)[None, :]) % samples) / samples
    even = gauss[:, None] * np.cos(turn)
    even[0] *= 0.5
    odd = gauss[:, None] * np.sin(turn)
    norms = []
    for band in range(BANDS):
        away = np.arange(samples) - (band + 0.5) * samples / BANDS
        window = np.where(np.abs(away) <= half, np.exp(-0.5 * (away / (samples / 8)) ** 2), 0.0)
        norms.append(float(1.0 / np.sum(window * window)))
    edge = float(np.exp(-0.5 * (half / (samples / 8)) ** 2))
    return np.stack([even, odd]).astype(ml_dtypes.bfloat16), norms, edge


def maps_kernel(
    norms, edge, strips, step, count, outer, gives_edge, waits, info, bias, x_hbm, scale_ref,
    table_hbm, *refs,
):
    refs = list(refs)
    ext_ref = refs.pop(0) if outer[0] or outer[1] else None
    if waits:
        refs.pop(0)
    send_ref, keep_ref = refs.pop(0), refs.pop(0)
    give_ref = refs.pop(0) if gives_edge else None
    rough_ref, struct_ref, x_ref, level_ref, near_ref, even_ref, odd_ref, sems, *scratch = refs
    lines = LANES
    samples = x_hbm.shape[-1]
    blocks = samples // LANES
    parts = lines // SUB
    rows = REPEATS * SUB
    flip = info[0]
    tile = jnp.where(flip == 1, count - 1 - step, step)
    lane = lax.broadcasted_iota(jnp.int32, (SUB, LANES), 1)
    mirror = jnp.where(lane == 0, 0, LANES - lane)
    sign = jnp.where(lane % 2 == 0, edge, -edge)

    line_count = x_hbm.shape[1]
    base = pl.multiple_of(tile * lines, lines)
    base_prev = pl.multiple_of(jnp.maximum(base - SUB, 0), SUB)
    base_next = pl.multiple_of(jnp.minimum(base + lines, line_count - SUB), SUB)
    first_copy = pltpu.make_async_copy(
        x_hbm.at[:, pl.ds(base, SUB), :], x_ref.at[:, :SUB, :], sems.at[0]
    )
    own = pltpu.make_async_copy(
        x_hbm.at[:, pl.ds(pl.multiple_of(base + SUB, SUB), lines - SUB), :],
        x_ref.at[:, SUB:lines, :],
        sems.at[5],
    )
    tables = [
        pltpu.make_async_copy(table_hbm.at[n], ref, sems.at[1 + n])
        for n, ref in enumerate((even_ref, odd_ref))
    ]
    starts = [base_prev, base_next]
    if gives_edge:
        base_give = pl.multiple_of(jnp.where(flip == 1, 0, line_count - SUB), SUB)
        starts.append(base_give)
    edges = [
        pltpu.make_async_copy(x_hbm.at[:, pl.ds(start, SUB), :], near_ref.at[n], sems.at[(3, 4, 6)[n]])
        for n, start in enumerate(starts)
    ]
    for copy in [first_copy] + tables + edges + [own]:
        copy.start()

    at_start, at_end = tile == 0, tile == count - 1
    whole_prev = pl.ds(pl.multiple_of(jnp.maximum(base - lines, 0), lines), lines)
    whole_next = pl.ds(pl.multiple_of(jnp.minimum(base + lines, line_count - lines), lines), lines)

    def placed(values, at):
        above = jnp.zeros((at, values.shape[1]), values.dtype)
        below = jnp.zeros((SUB - 2 - at, values.shape[1]), values.dtype)
        return jnp.concatenate([piece for piece in (above, values, below) if piece.shape[0]], axis=0)

    row_of = lax.broadcasted_iota(jnp.int32, (SUB, blocks), 0)
    for r in range(REPEATS):
        level_ref[r, :lines, :] = scale_ref[r, :, pl.ds(base, lines)].T
        level_prev = scale_ref[r, :, whole_prev].T[lines - SUB :]
        level_next = scale_ref[r, :, whole_next].T[:SUB]
        if outer[0] or outer[1]:
            outside = ext_ref[2 * r : 2 * r + 2, samples : samples + blocks]
        if outer[0]:
            level_prev = jnp.where(at_start, placed(outside, SUB - 2), level_prev)
        if outer[1]:
            level_next = jnp.where(at_end, placed(outside, 0), level_next)
        level_ref[r, lines:, :] = jnp.where(row_of < 2, level_next, level_prev)

    def fold(s, buffers):
        even_in, odd_in, edge_in = buffers
        for r in range(REPEATS):
            at = pl.ds(pl.multiple_of(s * SUB, SUB), SUB)
            level = level_ref[r, at, :]
            values = [
                x_ref[r, at, kb * LANES : (kb + 1) * LANES].astype(jnp.float32)
                * level[:, kb : kb + 1]
                for kb in range(blocks)
            ]
            forward = [v.astype(jnp.bfloat16) for v in values]
            turned = [
                jnp.take_along_axis(v, mirror, axis=1, mode="promise_in_bounds") for v in values
            ]
            zero = jnp.zeros((SUB, LANES), jnp.float32)
            backward = []
            for i in range(blocks + 1):
                first = turned[blocks - i] if i > 0 else zero
                rest = turned[blocks - 1 - i] if i < blocks else zero
                backward.append(jnp.where(lane == 0, first, rest).astype(jnp.bfloat16))
            span = blocks // BANDS
            for band in range(BANDS):
                to = slice(band * rows + r * SUB, band * rows + r * SUB + SUB)
                centre = span // 2 + span * band
                for i in range(blocks // 2):
                    ahead = forward[centre + i] if centre + i < blocks else None
                    j = blocks - centre + i
                    behind = backward[j] if j <= blocks else None
                    if behind is None:
                        plus, minus = ahead, ahead
                    elif ahead is None:
                        plus, minus = behind, -behind
                    else:
                        plus, minus = ahead + behind, ahead - behind
                    even_in[to, i * LANES : (i + 1) * LANES] = plus
                    odd_in[to, i * LANES : (i + 1) * LANES] = minus
                far = centre + blocks // 2
                far = far if far < blocks else centre - blocks // 2
                edge_in[to, :] = forward[far].astype(jnp.float32)[:, :1] * sign

    def limits(t):
        return info[2 + 2 * t], info[3 + 2 * t]

    first, last = limits(tile)
    prev_first, prev_last = limits(jnp.maximum(tile - 1, 0))
    next_first, next_last = limits(jnp.minimum(tile + 1, count - 1))
    out_at = 2 + 3 * count
    prev_first = jnp.where(at_start, info[out_at] if outer[0] else 1 << 20, prev_first)
    prev_last = jnp.where(at_start, info[out_at + 1] if outer[0] else -1, prev_last)
    next_first = jnp.where(at_end, info[out_at + 2] if outer[1] else 1 << 20, next_first)
    next_last = jnp.where(at_end, info[out_at + 3] if outer[1] else -1, next_last)

    def shut(values, low, high, at=0):
        out = []
        for n in range(values.shape[1] // LANES):
            inside = jnp.logical_and(low <= at + n, at + n <= high)
            out.append(jnp.where(inside, values[:, n * LANES : (n + 1) * LANES], 0.0))
        return jnp.concatenate(out, axis=1)

    def finish(powers_of):
        ratio, total = None, None
        for band in range(BANDS):
            powers = [powers_of(band, r) for r in range(REPEATS)]
            level = (powers[0] + powers[1]) + (powers[2] + powers[3])
            level = level * (norms[band] / (BANDS * REPEATS))
            total = level if total is None else total + level
            for p, q in zip(powers[:-1], powers[1:]):
                product, both = p * q, p + q
                part = product * lax.rsqrt(product * (both * both))
                ratio = part if ratio is None else ratio + part
        rough = 1.0 - ratio * (2.0 / (BANDS * (REPEATS - 1)))
        return rough, jnp.log(total + 0.05)

    def dots(s, buffers, border):
        even_in, odd_in, edge_in = buffers
        wide = DEPTH // SPLIT
        for part in range(SPLIT):
            columns = slice(part * wide, (part + 1) * wide)
            re = jnp.dot(even_in[...], even_ref[:, columns], preferred_element_type=jnp.float32)
            im = jnp.dot(odd_in[...], odd_ref[:, columns], preferred_element_type=jnp.float32)
            block0 = part * (wide // LANES)
            for g in range(SUB // 8):

                def power(band, r):
                    at = slice(band * rows + r * SUB + g * 8, band * rows + r * SUB + g * 8 + 8)
                    extra = jnp.concatenate([edge_in[at]] * (wide // LANES), axis=1)
                    a, b = re[at] + extra, im[at]
                    return a * a + b * b + 0.05 / norms[band]

                rough, struct = finish(power)
                if border:
                    rough_ref[g * 8 : g * 8 + 8, columns] = shut(rough, prev_first, prev_last, block0)
                    at = SUB + lines + g * 8
                    rough_ref[at : at + 8, columns] = shut(rough, next_first, next_last, block0)
                else:
                    line0 = pl.multiple_of(s * SUB + g * 8, 8)
                    rough_ref[pl.ds(line0 + SUB, 8), columns] = shut(rough, first, last, block0)
                    struct_ref[pl.ds(line0, 8), columns] = struct

    bufs = [scratch[0:3], scratch[3:6]]
    first_copy.wait()
    fold(0, bufs[0])
    for copy in [own] + edges + tables:
        copy.wait()
    for r in range(REPEATS):
        for kb in range(blocks):
            columns = slice(kb * LANES, (kb + 1) * LANES)
            a = near_ref[0, r, :, columns].astype(jnp.float32)
            b = near_ref[1, r, :, columns].astype(jnp.float32)
            if outer[0]:
                a = jnp.where(at_start, placed(ext_ref[2 * r : 2 * r + 2, columns], SUB - 2), a)
            if outer[1]:
                b = jnp.where(at_end, placed(ext_ref[2 * r : 2 * r + 2, columns], 0), b)
            low = lax.broadcasted_iota(jnp.int32, (SUB, LANES), 0) < 2
            x_ref[r, lines:, columns] = jnp.where(low, b, a).astype(jnp.bfloat16)

    if gives_edge:
        give_cols = pl.ds(pl.multiple_of(jnp.where(flip == 1, 0, line_count - lines), lines), lines)
        give_tile = jnp.where(flip == 1, 0, count - 1)
        for r in range(REPEATS):
            at = slice(2 * r, 2 * r + 2)
            for kb in range(blocks):
                columns = slice(kb * LANES, (kb + 1) * LANES)
                piece = near_ref[2, r, :, columns].astype(jnp.float32)
                give_ref[at, columns] = jnp.where(flip == 1, piece[:2], piece[SUB - 2 :])
            level = scale_ref[r, :, give_cols].T
            level = jnp.where(flip == 1, level[:2], level[lines - 2 :])
            edge_first = info[2 + 2 * give_tile].astype(jnp.float32)
            edge_last = info[3 + 2 * give_tile].astype(jnp.float32)
            give_ref[at, samples:] = jnp.concatenate(
                [
                    level,
                    jnp.full((2, 1), edge_first, jnp.float32),
                    jnp.full((2, 1), edge_last, jnp.float32),
                    jnp.zeros((2, LANES - blocks - 2), jnp.float32),
                ],
                axis=1,
            )


    def pair(i, carry):
        dots(2 * i, bufs[0], False)
        fold(2 * i + 1, bufs[1])
        dots(2 * i + 1, bufs[1], False)
        fold(2 * i + 2, bufs[0])
        return carry

    lax.fori_loop(0, parts // 2, pair, 0)
    dots(parts, bufs[0], True)

    pick = info[2 + 2 * count + tile]
    chosen = struct_ref[:, pl.ds(pl.multiple_of(pick * LANES, LANES), LANES)]
    score = jnp.sum(chosen) * (1.0 / (LANES * lines)) + bias[tile]
    smooth = TAPS[0] * rough_ref[SUB - 2 : SUB - 2 + lines, :]
    for k in range(1, 5):
        smooth = smooth + TAPS[k] * rough_ref[SUB - 2 + k : SUB - 2 + k + lines, :]
    maps = (smooth, shut(struct_ref[...], first, last))
    half = (send_ref.shape[0] - 8) // 2
    strip = DEPTH // strips
    low = info[1] % 2 == 0
    for m, whole in enumerate(maps):
        for zb in range(DEPTH // LANES):
            block = whole[:, zb * LANES : (zb + 1) * LANES].T
            for s in range(LANES // (2 * strip)):
                a = block[2 * s * strip : (2 * s + 1) * strip]
                b = block[(2 * s + 1) * strip : (2 * s + 2) * strip]
                at = m * half + zb * (LANES // 2) + s * strip
                keep_ref[at : at + strip, :] = jnp.where(low, a, b)
                send_ref[at : at + strip, :] = jnp.where(low, b, a)
    row = jnp.full((8, lines), score, jnp.float32)
    keep_ref[2 * half :, :] = row
    send_ref[2 * half :, :] = row


SUB = 16
SPLIT = 2


def maps_call(step, count, outer, gives_edge, info, bias, spectra, scales, extra, table, norms, edge, strips):
    samples = spectra.shape[-1]
    rows = BANDS * REPEATS * SUB
    out = jax.ShapeDtypeStruct((DEPTH + 8, LANES), jnp.float32)
    half = samples // 2
    whole = pl.BlockSpec(memory_space=pltpu.VMEM)
    remote = pl.BlockSpec(memory_space=pltpu.HBM)
    scales = jnp.swapaxes(scales, 1, 2)
    has_ext = outer[0] or outer[1]
    waits = len(extra) > has_ext
    outs = [out, out]
    if gives_edge:
        outs.append(jax.ShapeDtypeStruct((2 * REPEATS, samples + LANES), jnp.float32))
    pair = [
        pltpu.VMEM((rows, half), jnp.bfloat16),
        pltpu.VMEM((rows, half), jnp.bfloat16),
        pltpu.VMEM((rows, LANES), jnp.float32),
    ]
    return pl.pallas_call(
        functools.partial(
            maps_kernel, norms, edge, strips, step, count, outer, gives_edge, waits
        ),
        in_specs=[pl.BlockSpec(memory_space=pltpu.SMEM)] * 2
        + [remote, whole, remote]
        + [whole] * has_ext + [pl.BlockSpec(memory_space=pl.ANY)] * waits,
        out_specs=[whole] * len(outs),
        scratch_shapes=[
            pltpu.VMEM((LANES + 2 * SUB, DEPTH), jnp.float32),
            pltpu.VMEM((LANES, DEPTH), jnp.float32),
            pltpu.VMEM((REPEATS, LANES + SUB, samples), jnp.bfloat16),
            pltpu.VMEM((REPEATS, LANES + SUB, samples // LANES), jnp.float32),
            pltpu.VMEM((3, REPEATS, SUB, samples), jnp.bfloat16),
            pltpu.VMEM((half, DEPTH), jnp.bfloat16),
            pltpu.VMEM((half, DEPTH), jnp.bfloat16),
            pltpu.SemaphoreType.DMA((7,)),
        ] + pair + pair,
        out_shape=outs,
        compiler_params=pltpu.CompilerParams(vmem_limit_bytes=25 * 1024 * 1024 * 5 // 2),
        name="maps",
    )(info, bias, spectra, scales, table, *extra)


def merge_kernel(rows, strip, shares, vol, keep_ref, recv_ref, *outs):
    top_a, top_b = keep_ref[2 * rows : 2 * rows + 8], recv_ref[2 * rows : 2 * rows + 8]
    top = jnp.maximum(top_a, top_b)
    wa, wb = jnp.exp(top_a - top), jnp.exp(top_b - top)
    row = lax.broadcasted_iota(jnp.int32, (8, LANES), 0)
    tail = jnp.where(row < 4, top, wa + wb)
    wa, wb = wa[:1], wb[:1]
    mine = vol[0] // 2
    for d in range(shares):
        t = jnp.bitwise_xor(mine, d)
        at = pl.ds(pl.multiple_of(t * strip, strip), strip)
        struct = pl.ds(pl.multiple_of(rows + t * strip, strip), strip)
        sa, sb = keep_ref[at, :], recv_ref[at, :]
        first, other = wa * sa, wb * sb
        outs[d][:strip] = first + other
        outs[d][strip : 2 * strip] = first * sa + other * sb
        outs[d][2 * strip : 3 * strip] = wa * keep_ref[struct, :] + wb * recv_ref[struct, :]
        outs[d][3 * strip :] = tail


def merge_call(vol, keep, recv, strips):
    strip, shares = DEPTH // strips, strips // 2
    whole = pl.BlockSpec(memory_space=pltpu.VMEM)
    out = jax.ShapeDtypeStruct((3 * strip + 8, LANES), jnp.float32)
    return pl.pallas_call(
        functools.partial(merge_kernel, DEPTH // 2, strip, shares),
        in_specs=[pl.BlockSpec(memory_space=pltpu.SMEM), whole, whole],
        out_specs=[whole] * shares,
        out_shape=[out] * shares,
        compiler_params=pltpu.CompilerParams(vmem_limit_bytes=4 * 1024 * 1024),
        name="merge",
    )(vol, keep, recv)


def final_kernel(strip, count, shares, info, *refs):
    parts, (angio_ref, joined_ref, spread_ref) = refs[: count * shares], refs[count * shares :]
    for i in range(count):
        mine = parts[i * shares : (i + 1) * shares]
        tops = [p[3 * strip : 3 * strip + 1] for p in mine]
        top = functools.reduce(jnp.maximum, tops)
        scales = [jnp.exp(t - top) for t in tops]
        weight = functools.reduce(
            lambda a, b: a + b, [w * p[3 * strip + 4 : 3 * strip + 5] for w, p in zip(scales, mine)]
        )
        scales = [w / weight for w in scales]
        mean, second, joined = (
            functools.reduce(
                lambda a, b: a + b,
                [w * p[m * strip : (m + 1) * strip] for w, p in zip(scales, mine)],
            )
            for m in range(3)
        )
        tile = jnp.where(info[0] == 1, count - 1 - i, i)
        columns = pl.ds(pl.multiple_of(tile * LANES, LANES), LANES)
        angio_ref[:, columns] = mean
        joined_ref[:, columns] = joined
        spread_ref[:, columns] = jnp.sqrt(second - mean * mean + 0.01)


def final_call(info, parts, count, strips):
    strip, shares = DEPTH // strips, strips // 2
    whole = pl.BlockSpec(memory_space=pltpu.VMEM)
    out = jax.ShapeDtypeStruct((strip, count * LANES), jnp.float32)
    return pl.pallas_call(
        functools.partial(final_kernel, strip, count, shares),
        in_specs=[pl.BlockSpec(memory_space=pltpu.SMEM)] + [whole] * len(parts),
        out_specs=[whole] * 3,
        out_shape=[out] * 3,
        compiler_params=pltpu.CompilerParams(vmem_limit_bytes=4 * 1024 * 1024),
        name="final",
    )(info, *parts)


def edge_rows(spectra, scales, start, block):
    lines = lax.dynamic_slice_in_dim(spectra, start, 2, axis=1).astype(jnp.float32)
    level = lax.dynamic_slice_in_dim(scales, start, 2, axis=1)
    rows = lines.shape[0] * 2
    limits = jnp.broadcast_to(block.astype(jnp.float32)[None], (rows, 2))
    rest = jnp.zeros((rows, LANES - level.shape[2] - 2), jnp.float32)
    return jnp.concatenate(
        [lines.reshape(rows, -1), level.reshape(rows, -1), limits, rest], axis=1
    )


def on_device(tiles, strips, spectra, scales, retina, quality, bias):
    spectra, scales, quality, bias = spectra[0], scales[0], quality[0], bias[0]
    samples = spectra.shape[-1]
    count = retina.shape[0]
    table, norms, edge = constants(samples)
    table = jnp.asarray(table)
    here = lax.axis_index("tile")
    vol = lax.axis_index("vol")
    lines = spectra.shape[1]

    at = samples + scales.shape[2]
    none = jnp.array([1 << 20, -1], jnp.int32)
    flip = (here == 1).astype(jnp.int32) if tiles == 2 else jnp.zeros((), jnp.int32)
    info = jnp.concatenate(
        [flip[None], vol[None].astype(jnp.int32), retina.reshape(-1), quality]
    ).astype(jnp.int32)

    def with_limits(before, after):
        before_block = jnp.where(here == 0, none, before[0, at : at + 2].astype(jnp.int32))
        after_block = jnp.where(here == tiles - 1, none, after[0, at : at + 2].astype(jnp.int32))
        return jnp.concatenate([info, before_block, after_block])

    if tiles == 2:
        outside = [(False, False)] * (count - 1) + [(True, True)]
    else:
        up = [(i, i + 1) for i in range(tiles - 1)]
        down = [(i + 1, i) for i in range(tiles - 1)]
        before = lax.ppermute(edge_rows(spectra, scales, lines - 2, retina[count - 1]), "tile", up)
        after = lax.ppermute(edge_rows(spectra, scales, 0, retina[0]), "tile", down)
        info = with_limits(before, after)
        outside = [(i == 0, i == count - 1) for i in range(count)]

    shares = strips // 2
    swap = [(v, v ^ 1) for v in range(strips)]
    kept, arrived, parts = [], [], []

    def merge(i):
        own, *rest = merge_call(vol[None], kept[i], arrived[i], strips)
        got = [
            lax.ppermute(p, "vol", [(v, v ^ (2 * d)) for v in range(strips)])
            for d, p in zip(range(1, shares), rest)
        ]
        parts.append([own] + got)

    for i in range(count):
        outer = outside[i]
        gives_edge = tiles == 2 and i == 0
        extra = []
        if outer[0] or outer[1]:
            if tiles == 2:
                after = lax.ppermute(given, "tile", [(0, 1), (1, 0)])
                step_info = with_limits(after, after)
            else:
                step_info = info
            extra.append(after if outer[1] else before)
        else:
            step_info = info
        if i >= 2:
            merge(i - 2)
            extra.append(parts[i - 2][0])
        send, keep, *rest = maps_call(
            i, count, outer, gives_edge, step_info, bias,
            spectra, scales, extra, table, norms, edge, strips,
        )
        if gives_edge:
            given = rest[0]
        kept.append(keep)
        arrived.append(lax.ppermute(send, "vol", swap))
    for i in range(max(count - 2, 0), count):
        merge(i)
    flat = [p for own in parts for p in own]
    return tuple(final_call(info, flat, count, strips))


def solution(mesh):
    return jax.shard_map(
        functools.partial(on_device, mesh.shape["tile"], mesh.shape["vol"]),
        mesh=mesh,
        in_specs=(
            P(("study", "vol"), None, "tile", None),
            P(("study", "vol"), None, "tile", None),
            P(("study", "tile"), None),
            P(("study", "vol"), "tile"),
            P(("study", "vol"), "tile"),
        ),
        out_specs=(P(("study", "vol"), "tile"),) * 3,
        check_vma=False,
    )
```

```python
import functools
import math

import jax
import jax.numpy as jnp
import ml_dtypes
import numpy as np
from jax import lax
from jax.experimental import pallas as pl
from jax.experimental.pallas import tpu as pltpu
from jax.sharding import PartitionSpec as P

DEPTH = 512
BANDS = 4
REPEATS = 4
LANES = 128
HALO = 8
TAPS = (1.0 / 9.0, 2.0 / 9.0, 3.0 / 9.0, 2.0 / 9.0, 1.0 / 9.0)


def constants(samples):
    half = samples // 2
    distance = np.arange(half, dtype=np.float64)
    gauss = np.exp(-0.5 * (distance / (samples / 8)) ** 2)
    turn = 2.0 * np.pi * ((np.arange(half)[:, None] * np.arange(DEPTH)[None, :]) % samples) / samples
    even = gauss[:, None] * np.cos(turn)
    even[0] *= 0.5
    odd = gauss[:, None] * np.sin(turn)
    norms = []
    for band in range(BANDS):
        away = np.arange(samples) - (band + 0.5) * samples / BANDS
        window = np.where(np.abs(away) <= half, np.exp(-0.5 * (away / (samples / 8)) ** 2), 0.0)
        norms.append(float(1.0 / np.sum(window * window)))
    edge = float(np.exp(-0.5 * (half / (samples / 8)) ** 2))
    return np.stack([even, odd]).astype(ml_dtypes.bfloat16), norms, edge


def maps_kernel(
    norms, edge, strips, step, count, outer, gives_edge, waits, info, bias, x_hbm, scale_ref,
    table_hbm, *refs,
):
    refs = list(refs)
    ext_ref = refs.pop(0) if outer[0] or outer[1] else None
    if waits:
        refs.pop(0)
    send_ref, keep_ref = refs.pop(0), refs.pop(0)
    give_ref = refs.pop(0) if gives_edge else None
    rough_ref, struct_ref, x_ref, level_ref, near_ref, even_ref, odd_ref, sems, *scratch = refs
    lines = LANES
    samples = x_hbm.shape[-1]
    blocks = samples // LANES
    parts = lines // SUB
    rows = REPEATS * SUB
    flip = info[0]
    tile = jnp.where(flip == 1, count - 1 - step, step)
    lane = lax.broadcasted_iota(jnp.int32, (SUB, LANES), 1)
    mirror = jnp.where(lane == 0, 0, LANES - lane)
    sign = jnp.where(lane % 2 == 0, edge, -edge)

    line_count = x_hbm.shape[1]
    base = pl.multiple_of(tile * lines, lines)
    base_prev = pl.multiple_of(jnp.maximum(base - SUB, 0), SUB)
    base_next = pl.multiple_of(jnp.minimum(base + lines, line_count - SUB), SUB)
    first_copy = pltpu.make_async_copy(
        x_hbm.at[:, pl.ds(base, SUB), :], x_ref.at[:, :SUB, :], sems.at[0]
    )
    own = pltpu.make_async_copy(
        x_hbm.at[:, pl.ds(pl.multiple_of(base + SUB, SUB), lines - SUB), :],
        x_ref.at[:, SUB:lines, :],
        sems.at[5],
    )
    tables = [
        pltpu.make_async_copy(table_hbm.at[n], ref, sems.at[1 + n])
        for n, ref in enumerate((even_ref, odd_ref))
    ]
    starts = [base_prev, base_next]
    if gives_edge:
        base_give = pl.multiple_of(jnp.where(flip == 1, 0, line_count - SUB), SUB)
        starts.append(base_give)
    edges = [
        pltpu.make_async_copy(x_hbm.at[:, pl.ds(start, SUB), :], near_ref.at[n], sems.at[(3, 4, 6)[n]])
        for n, start in enumerate(starts)
    ]
    for copy in [first_copy] + tables + edges + [own]:
        copy.start()

    at_start, at_end = tile == 0, tile == count - 1
    whole_prev = pl.ds(pl.multiple_of(jnp.maximum(base - lines, 0), lines), lines)
    whole_next = pl.ds(pl.multiple_of(jnp.minimum(base + lines, line_count - lines), lines), lines)

    def placed(values, at):
        above = jnp.zeros((at, values.shape[1]), values.dtype)
        below = jnp.zeros((SUB - 2 - at, values.shape[1]), values.dtype)
        return jnp.concatenate([piece for piece in (above, values, below) if piece.shape[0]], axis=0)

    row_of = lax.broadcasted_iota(jnp.int32, (SUB, blocks), 0)
    for r in range(REPEATS):
        level_ref[r, :lines, :] = scale_ref[r, :, pl.ds(base, lines)].T
        level_prev = scale_ref[r, :, whole_prev].T[lines - SUB :]
        level_next = scale_ref[r, :, whole_next].T[:SUB]
        if outer[0] or outer[1]:
            outside = ext_ref[2 * r : 2 * r + 2, samples : samples + blocks]
        if outer[0]:
            level_prev = jnp.where(at_start, placed(outside, SUB - 2), level_prev)
        if outer[1]:
            level_next = jnp.where(at_end, placed(outside, 0), level_next)
        level_ref[r, lines:, :] = jnp.where(row_of < 2, level_next, level_prev)

    def fold(s, buffers):
        even_in, odd_in, edge_in = buffers
        for r in range(REPEATS):
            at = pl.ds(pl.multiple_of(s * SUB, SUB), SUB)
            level = level_ref[r, at, :]
            values = [
                x_ref[r, at, kb * LANES : (kb + 1) * LANES].astype(jnp.float32)
                * level[:, kb : kb + 1]
                for kb in range(blocks)
            ]
            forward = [v.astype(jnp.bfloat16) for v in values]
            turned = [
                jnp.take_along_axis(v, mirror, axis=1, mode="promise_in_bounds") for v in values
            ]
            zero = jnp.zeros((SUB, LANES), jnp.float32)
            backward = []
            for i in range(blocks + 1):
                first = turned[blocks - i] if i > 0 else zero
                rest = turned[blocks - 1 - i] if i < blocks else zero
                backward.append(jnp.where(lane == 0, first, rest).astype(jnp.bfloat16))
            span = blocks // BANDS
            for band in range(BANDS):
                to = slice(band * rows + r * SUB, band * rows + r * SUB + SUB)
                centre = span // 2 + span * band
                for i in range(blocks // 2):
                    ahead = forward[centre + i] if centre + i < blocks else None
                    j = blocks - centre + i
                    behind = backward[j] if j <= blocks else None
                    if behind is None:
                        plus, minus = ahead, ahead
                    elif ahead is None:
                        plus, minus = behind, -behind
                    else:
                        plus, minus = ahead + behind, ahead - behind
                    even_in[to, i * LANES : (i + 1) * LANES] = plus
                    odd_in[to, i * LANES : (i + 1) * LANES] = minus
                far = centre + blocks // 2
                far = far if far < blocks else centre - blocks // 2
                edge_in[to, :] = forward[far].astype(jnp.float32)[:, :1] * sign

    def limits(t):
        return info[2 + 2 * t], info[3 + 2 * t]

    first, last = limits(tile)
    prev_first, prev_last = limits(jnp.maximum(tile - 1, 0))
    next_first, next_last = limits(jnp.minimum(tile + 1, count - 1))
    out_at = 2 + 3 * count
    prev_first = jnp.where(at_start, info[out_at] if outer[0] else 1 << 20, prev_first)
    prev_last = jnp.where(at_start, info[out_at + 1] if outer[0] else -1, prev_last)
    next_first = jnp.where(at_end, info[out_at + 2] if outer[1] else 1 << 20, next_first)
    next_last = jnp.where(at_end, info[out_at + 3] if outer[1] else -1, next_last)

    def shut(values, low, high, at=0):
        out = []
        for n in range(values.shape[1] // LANES):
            inside = jnp.logical_and(low <= at + n, at + n <= high)
            out.append(jnp.where(inside, values[:, n * LANES : (n + 1) * LANES], 0.0))
        return jnp.concatenate(out, axis=1)

    def finish(powers_of):
        ratio, total = None, None
        for band in range(BANDS):
            powers = [powers_of(band, r) for r in range(REPEATS)]
            level = (powers[0] + powers[1]) + (powers[2] + powers[3])
            level = level * (norms[band] / (BANDS * REPEATS))
            total = level if total is None else total + level
            for p, q in zip(powers[:-1], powers[1:]):
                product, both = p * q, p + q
                part = product * lax.rsqrt(product * (both * both))
                ratio = part if ratio is None else ratio + part
        rough = 1.0 - ratio * (2.0 / (BANDS * (REPEATS - 1)))
        return rough, jnp.log(total + 0.05)

    def dots(s, buffers, border):
        even_in, odd_in, edge_in = buffers
        wide = DEPTH // SPLIT
        for part in range(SPLIT):
            columns = slice(part * wide, (part + 1) * wide)
            re = jnp.dot(even_in[...], even_ref[:, columns], preferred_element_type=jnp.float32)
            im = jnp.dot(odd_in[...], odd_ref[:, columns], preferred_element_type=jnp.float32)
            block0 = part * (wide // LANES)
            for g in range(SUB // 8):

                def power(band, r):
                    at = slice(band * rows + r * SUB + g * 8, band * rows + r * SUB + g * 8 + 8)
                    extra = jnp.concatenate([edge_in[at]] * (wide // LANES), axis=1)
                    a, b = re[at] + extra, im[at]
                    return a * a + b * b + 0.05 / norms[band]

                rough, struct = finish(power)
                if border:
                    rough_ref[g * 8 : g * 8 + 8, columns] = shut(rough, prev_first, prev_last, block0)
                    at = SUB + lines + g * 8
                    rough_ref[at : at + 8, columns] = shut(rough, next_first, next_last, block0)
                else:
                    line0 = pl.multiple_of(s * SUB + g * 8, 8)
                    rough_ref[pl.ds(line0 + SUB, 8), columns] = shut(rough, first, last, block0)
                    struct_ref[pl.ds(line0, 8), columns] = struct

    bufs = [scratch[0:3], scratch[3:6]]
    first_copy.wait()
    fold(0, bufs[0])
    for copy in [own] + edges + tables:
        copy.wait()
    for r in range(REPEATS):
        for kb in range(blocks):
            columns = slice(kb * LANES, (kb + 1) * LANES)
            a = near_ref[0, r, :, columns].astype(jnp.float32)
            b = near_ref[1, r, :, columns].astype(jnp.float32)
            if outer[0]:
                a = jnp.where(at_start, placed(ext_ref[2 * r : 2 * r + 2, columns], SUB - 2), a)
            if outer[1]:
                b = jnp.where(at_end, placed(ext_ref[2 * r : 2 * r + 2, columns], 0), b)
            low = lax.broadcasted_iota(jnp.int32, (SUB, LANES), 0) < 2
            x_ref[r, lines:, columns] = jnp.where(low, b, a).astype(jnp.bfloat16)

    if gives_edge:
        give_cols = pl.ds(pl.multiple_of(jnp.where(flip == 1, 0, line_count - lines), lines), lines)
        give_tile = jnp.where(flip == 1, 0, count - 1)
        for r in range(REPEATS):
            at = slice(2 * r, 2 * r + 2)
            for kb in range(blocks):
                columns = slice(kb * LANES, (kb + 1) * LANES)
                piece = near_ref[2, r, :, columns].astype(jnp.float32)
                give_ref[at, columns] = jnp.where(flip == 1, piece[:2], piece[SUB - 2 :])
            level = scale_ref[r, :, give_cols].T
            level = jnp.where(flip == 1, level[:2], level[lines - 2 :])
            edge_first = info[2 + 2 * give_tile].astype(jnp.float32)
            edge_last = info[3 + 2 * give_tile].astype(jnp.float32)
            give_ref[at, samples:] = jnp.concatenate(
                [
                    level,
                    jnp.full((2, 1), edge_first, jnp.float32),
                    jnp.full((2, 1), edge_last, jnp.float32),
                    jnp.zeros((2, LANES - blocks - 2), jnp.float32),
                ],
                axis=1,
            )


    def pair(i, carry):
        dots(2 * i, bufs[0], False)
        fold(2 * i + 1, bufs[1])
        dots(2 * i + 1, bufs[1], False)
        fold(2 * i + 2, bufs[0])
        return carry

    lax.fori_loop(0, parts // 2, pair, 0)
    dots(parts, bufs[0], True)

    pick = info[2 + 2 * count + tile]
    chosen = struct_ref[:, pl.ds(pl.multiple_of(pick * LANES, LANES), LANES)]
    score = jnp.sum(chosen) * (1.0 / (LANES * lines)) + bias[tile]
    smooth = TAPS[0] * rough_ref[SUB - 2 : SUB - 2 + lines, :]
    for k in range(1, 5):
        smooth = smooth + TAPS[k] * rough_ref[SUB - 2 + k : SUB - 2 + k + lines, :]
    maps = (smooth, shut(struct_ref[...], first, last))
    half = (send_ref.shape[0] - 8) // 2
    strip = DEPTH // strips
    low = info[1] % 2 == 0
    for m, whole in enumerate(maps):
        for zb in range(DEPTH // LANES):
            block = whole[:, zb * LANES : (zb + 1) * LANES].T
            for s in range(LANES // (2 * strip)):
                a = block[2 * s * strip : (2 * s + 1) * strip]
                b = block[(2 * s + 1) * strip : (2 * s + 2) * strip]
                at = m * half + zb * (LANES // 2) + s * strip
                keep_ref[at : at + strip, :] = jnp.where(low, a, b)
                send_ref[at : at + strip, :] = jnp.where(low, b, a)
    row = jnp.full((8, lines), score, jnp.float32)
    keep_ref[2 * half :, :] = row
    send_ref[2 * half :, :] = row


SUB = 16
SPLIT = 2


def maps_call(step, count, outer, gives_edge, info, bias, spectra, scales, extra, table, norms, edge, strips):
    samples = spectra.shape[-1]
    rows = BANDS * REPEATS * SUB
    out = jax.ShapeDtypeStruct((DEPTH + 8, LANES), jnp.float32)
    half = samples // 2
    whole = pl.BlockSpec(memory_space=pltpu.VMEM)
    remote = pl.BlockSpec(memory_space=pltpu.HBM)
    scales = jnp.swapaxes(scales, 1, 2)
    has_ext = outer[0] or outer[1]
    waits = len(extra) > has_ext
    outs = [out, out]
    if gives_edge:
        outs.append(jax.ShapeDtypeStruct((2 * REPEATS, samples + LANES), jnp.float32))
    pair = [
        pltpu.VMEM((rows, half), jnp.bfloat16),
        pltpu.VMEM((rows, half), jnp.bfloat16),
        pltpu.VMEM((rows, LANES), jnp.float32),
    ]
    return pl.pallas_call(
        functools.partial(
            maps_kernel, norms, edge, strips, step, count, outer, gives_edge, waits
        ),
        in_specs=[pl.BlockSpec(memory_space=pltpu.SMEM)] * 2
        + [remote, whole, remote]
        + [whole] * has_ext + [pl.BlockSpec(memory_space=pl.ANY)] * waits,
        out_specs=[whole] * len(outs),
        scratch_shapes=[
            pltpu.VMEM((LANES + 2 * SUB, DEPTH), jnp.float32),
            pltpu.VMEM((LANES, DEPTH), jnp.float32),
            pltpu.VMEM((REPEATS, LANES + SUB, samples), jnp.bfloat16),
            pltpu.VMEM((REPEATS, LANES + SUB, samples // LANES), jnp.float32),
            pltpu.VMEM((3, REPEATS, SUB, samples), jnp.bfloat16),
            pltpu.VMEM((half, DEPTH), jnp.bfloat16),
            pltpu.VMEM((half, DEPTH), jnp.bfloat16),
            pltpu.SemaphoreType.DMA((7,)),
        ] + pair + pair,
        out_shape=outs,
        compiler_params=pltpu.CompilerParams(vmem_limit_bytes=25 * 1024 * 1024 * 5 // 2),
        cost_estimate=pl.CostEstimate(
            flops=5 * BANDS * REPEATS * (LANES + SUB) * samples * DEPTH,
            bytes_accessed=2 * REPEATS * LANES * samples + 4 * samples * DEPTH,
            transcendentals=0,
        ),
        name="maps",
    )(info, bias, spectra, scales, table, *extra)


def merge_kernel(rows, strip, shares, tied, vol, keep_ref, recv_ref, *outs):
    outs = outs[len(outs) - shares - tied : len(outs) - tied]
    top_a, top_b = keep_ref[2 * rows : 2 * rows + 8], recv_ref[2 * rows : 2 * rows + 8]
    top = jnp.maximum(top_a, top_b)
    wa, wb = jnp.exp(top_a - top), jnp.exp(top_b - top)
    row = lax.broadcasted_iota(jnp.int32, (8, LANES), 0)
    tail = jnp.where(row < 4, top, wa + wb)
    wa, wb = wa[:1], wb[:1]
    mine = vol[0] // 2
    for d in range(shares):
        t = jnp.bitwise_xor(mine, d)
        at = pl.ds(pl.multiple_of(t * strip, strip), strip)
        struct = pl.ds(pl.multiple_of(rows + t * strip, strip), strip)
        sa, sb = keep_ref[at, :], recv_ref[at, :]
        first, other = wa * sa, wb * sb
        outs[d][:strip] = first + other
        outs[d][strip : 2 * strip] = first * sa + other * sb
        outs[d][2 * strip : 3 * strip] = wa * keep_ref[struct, :] + wb * recv_ref[struct, :]
        outs[d][3 * strip :] = tail


def merge_call(vol, keep, recv, later, strips):
    strip, shares = DEPTH // strips, strips // 2
    whole = pl.BlockSpec(memory_space=pltpu.VMEM)
    remote = pl.BlockSpec(memory_space=pl.ANY)
    out = jax.ShapeDtypeStruct((3 * strip + 8, LANES), jnp.float32)
    tied = [jax.ShapeDtypeStruct(a.shape, a.dtype) for a in later[:1]]
    return pl.pallas_call(
        functools.partial(merge_kernel, DEPTH // 2, strip, shares, len(tied)),
        in_specs=[pl.BlockSpec(memory_space=pltpu.SMEM), whole, whole] + [remote] * len(later),
        out_specs=[whole] * shares + [remote] * len(tied),
        out_shape=[out] * shares + tied,
        input_output_aliases={3: shares} if tied else {},
        compiler_params=pltpu.CompilerParams(vmem_limit_bytes=4 * 1024 * 1024),
        name="merge",
    )(vol, keep, recv, *later)


def final_kernel(strip, count, shares, info, *refs):
    parts, (angio_ref, joined_ref, spread_ref) = refs[: count * shares], refs[count * shares :]
    for i in range(count):
        mine = parts[i * shares : (i + 1) * shares]
        tops = [p[3 * strip : 3 * strip + 1] for p in mine]
        top = functools.reduce(jnp.maximum, tops)
        scales = [jnp.exp(t - top) for t in tops]
        weight = functools.reduce(
            lambda a, b: a + b, [w * p[3 * strip + 4 : 3 * strip + 5] for w, p in zip(scales, mine)]
        )
        scales = [w / weight for w in scales]
        mean, second, joined = (
            functools.reduce(
                lambda a, b: a + b,
                [w * p[m * strip : (m + 1) * strip] for w, p in zip(scales, mine)],
            )
            for m in range(3)
        )
        tile = jnp.where(info[0] == 1, count - 1 - i, i)
        columns = pl.ds(pl.multiple_of(tile * LANES, LANES), LANES)
        angio_ref[:, columns] = mean
        joined_ref[:, columns] = joined
        spread_ref[:, columns] = jnp.sqrt(second - mean * mean + 0.01)


def final_call(info, parts, count, strips):
    strip, shares = DEPTH // strips, strips // 2
    whole = pl.BlockSpec(memory_space=pltpu.VMEM)
    out = jax.ShapeDtypeStruct((strip, count * LANES), jnp.float32)
    return pl.pallas_call(
        functools.partial(final_kernel, strip, count, shares),
        in_specs=[pl.BlockSpec(memory_space=pltpu.SMEM)] + [whole] * len(parts),
        out_specs=[whole] * 3,
        out_shape=[out] * 3,
        compiler_params=pltpu.CompilerParams(vmem_limit_bytes=4 * 1024 * 1024),
        name="final",
    )(info, *parts)


def edge_rows(spectra, scales, start, block):
    lines = lax.dynamic_slice_in_dim(spectra, start, 2, axis=1).astype(jnp.float32)
    level = lax.dynamic_slice_in_dim(scales, start, 2, axis=1)
    rows = lines.shape[0] * 2
    limits = jnp.broadcast_to(block.astype(jnp.float32)[None], (rows, 2))
    rest = jnp.zeros((rows, LANES - level.shape[2] - 2), jnp.float32)
    return jnp.concatenate(
        [lines.reshape(rows, -1), level.reshape(rows, -1), limits, rest], axis=1
    )


def on_device(tiles, strips, spectra, scales, retina, quality, bias):
    spectra, scales, quality, bias = spectra[0], scales[0], quality[0], bias[0]
    samples = spectra.shape[-1]
    count = retina.shape[0]
    table, norms, edge = constants(samples)
    table = jnp.asarray(table)
    here = lax.axis_index("tile")
    vol = lax.axis_index("vol")
    lines = spectra.shape[1]

    at = samples + scales.shape[2]
    none = jnp.array([1 << 20, -1], jnp.int32)
    flip = (here == 1).astype(jnp.int32) if tiles == 2 else jnp.zeros((), jnp.int32)
    info = jnp.concatenate(
        [flip[None], vol[None].astype(jnp.int32), retina.reshape(-1), quality]
    ).astype(jnp.int32)

    def with_limits(before, after):
        before_block = jnp.where(here == 0, none, before[0, at : at + 2].astype(jnp.int32))
        after_block = jnp.where(here == tiles - 1, none, after[0, at : at + 2].astype(jnp.int32))
        return jnp.concatenate([info, before_block, after_block])

    if tiles == 2:
        outside = [(False, False)] * (count - 1) + [(True, True)]
    else:
        up = [(i, i + 1) for i in range(tiles - 1)]
        down = [(i + 1, i) for i in range(tiles - 1)]
        before = lax.ppermute(edge_rows(spectra, scales, lines - 2, retina[count - 1]), "tile", up)
        after = lax.ppermute(edge_rows(spectra, scales, 0, retina[0]), "tile", down)
        info = with_limits(before, after)
        outside = [(i == 0, i == count - 1) for i in range(count)]

    shares = strips // 2
    swap = [(v, v ^ 1) for v in range(strips)]
    kept, arrived, parts = [], [], []

    def merge(i, later):
        outs = merge_call(vol[None], kept[i], arrived[i], later, strips)
        got = [
            lax.ppermute(p, "vol", [(v, v ^ (2 * d)) for v in range(strips)])
            for d, p in zip(range(1, shares), outs[1:])
        ]
        parts.append([outs[0]] + got)
        return outs[-1]

    for i in range(count):
        outer = outside[i]
        gives_edge = tiles == 2 and i == 0
        extra = []
        if outer[0] or outer[1]:
            if tiles == 2:
                after = lax.ppermute(given, "tile", [(0, 1), (1, 0)])
                step_info = with_limits(after, after)
            else:
                step_info = info
            extra.append(after if outer[1] else before)
        else:
            step_info = info
        if i >= 2:
            if i == 2:
                merge(0, [])
            extra.append(parts[i - 2][0])
        send, keep, *rest = maps_call(
            i, count, outer, gives_edge, step_info, bias,
            spectra, scales, extra, table, norms, edge, strips,
        )
        if gives_edge:
            given = rest[0]
        kept.append(keep)
        if i >= 2:
            send = merge(i - 1, [send] + parts[i - 2][1:])
        arrived.append(lax.ppermute(send, "vol", swap))
    for i in range(len(parts), count):
        merge(i, [])
    flat = [p for own in parts for p in own]
    return tuple(final_call(info, flat, count, strips))


def solution(mesh):
    return jax.shard_map(
        functools.partial(on_device, mesh.shape["tile"], mesh.shape["vol"]),
        mesh=mesh,
        in_specs=(
            P(("study", "vol"), None, "tile", None),
            P(("study", "vol"), None, "tile", None),
            P(("study", "tile"), None),
            P(("study", "vol"), "tile"),
            P(("study", "vol"), "tile"),
        ),
        out_specs=(P(("study", "vol"), "tile"),) * 3,
        check_vma=False,
    )
```

```python
import functools
import math

import jax
import jax.numpy as jnp
import ml_dtypes
import numpy as np
from jax import lax
from jax.experimental import pallas as pl
from jax.experimental.pallas import tpu as pltpu
from jax.sharding import PartitionSpec as P

DEPTH = 512
BANDS = 4
REPEATS = 4
LANES = 128
HALO = 8
TAPS = (1.0 / 9.0, 2.0 / 9.0, 3.0 / 9.0, 2.0 / 9.0, 1.0 / 9.0)


def constants(samples):
    half = samples // 2
    distance = np.arange(half, dtype=np.float64)
    gauss = np.exp(-0.5 * (distance / (samples / 8)) ** 2)
    turn = 2.0 * np.pi * ((np.arange(half)[:, None] * np.arange(DEPTH)[None, :]) % samples) / samples
    even = gauss[:, None] * np.cos(turn)
    even[0] *= 0.5
    odd = gauss[:, None] * np.sin(turn)
    norms = []
    for band in range(BANDS):
        away = np.arange(samples) - (band + 0.5) * samples / BANDS
        window = np.where(np.abs(away) <= half, np.exp(-0.5 * (away / (samples / 8)) ** 2), 0.0)
        norms.append(float(1.0 / np.sum(window * window)))
    edge = float(np.exp(-0.5 * (half / (samples / 8)) ** 2))
    return np.stack([even, odd]).astype(ml_dtypes.bfloat16), norms, edge


class Whole:
    def __init__(self, ref):
        self.ref = ref

    def __getitem__(self, at):
        return self.ref[at].astype(jnp.int32)


def maps_kernel(
    norms, edge, strips, step, count, outer, gives_edge, waits, near_tables, values, x_hbm, scale_ref,
    table_in, *refs,
):
    refs = list(refs)
    ext_ref = refs.pop(0) if outer[0] or outer[1] else None
    if waits:
        refs.pop(0)
    send_ref, keep_ref = refs.pop(0), refs.pop(0)
    give_ref = refs.pop(0) if gives_edge else None
    rough_ref, struct_ref, x_ref, level_ref, near_ref, sems = refs[:6]
    scratch = refs[6:]
    if not near_tables:
        table_ref = scratch.pop()
    lines = LANES
    samples = x_hbm.shape[-1]
    blocks = samples // LANES
    parts = lines // SUB
    rows = REPEATS * SUB
    info = Whole(values)
    flip = info[0]
    tile = jnp.where(flip == 1, count - 1 - step, step)
    lane = lax.broadcasted_iota(jnp.int32, (SUB, LANES), 1)
    mirror = jnp.where(lane == 0, 0, LANES - lane)
    sign = jnp.where(lane % 2 == 0, edge, -edge)

    line_count = x_hbm.shape[1]
    base = pl.multiple_of(tile * lines, lines)
    base_prev = pl.multiple_of(jnp.maximum(base - SUB, 0), SUB)
    base_next = pl.multiple_of(jnp.minimum(base + lines, line_count - SUB), SUB)
    first_copy = pltpu.make_async_copy(
        x_hbm.at[:, pl.ds(base, SUB), :], x_ref.at[:, :SUB, :], sems.at[0]
    )
    own = pltpu.make_async_copy(
        x_hbm.at[:, pl.ds(pl.multiple_of(base + SUB, SUB), lines - SUB), :],
        x_ref.at[:, SUB:lines, :],
        sems.at[5],
    )
    tables = []
    if near_tables:
        even_ref, odd_ref = table_in.at[0], table_in.at[1]
    else:
        even_ref, odd_ref = table_ref.at[0], table_ref.at[1]
        tables.append(pltpu.make_async_copy(table_in, table_ref, sems.at[1]))
    starts = [base_prev, base_next]
    if gives_edge:
        base_give = pl.multiple_of(jnp.where(flip == 1, 0, line_count - SUB), SUB)
        starts.append(base_give)
    edges = [
        pltpu.make_async_copy(x_hbm.at[:, pl.ds(start, SUB), :], near_ref.at[n], sems.at[(3, 4, 6)[n]])
        for n, start in enumerate(starts)
    ]
    for copy in [first_copy] + tables + edges + [own]:
        copy.start()

    at_start, at_end = tile == 0, tile == count - 1
    whole_prev = pl.ds(pl.multiple_of(jnp.maximum(base - lines, 0), lines), lines)
    whole_next = pl.ds(pl.multiple_of(jnp.minimum(base + lines, line_count - lines), lines), lines)

    def placed(values, at):
        above = jnp.zeros((at, values.shape[1]), values.dtype)
        below = jnp.zeros((SUB - 2 - at, values.shape[1]), values.dtype)
        return jnp.concatenate([piece for piece in (above, values, below) if piece.shape[0]], axis=0)

    row_of = lax.broadcasted_iota(jnp.int32, (SUB, blocks), 0)
    for r in range(REPEATS):
        level_ref[r, :lines, :] = scale_ref[r, :, pl.ds(base, lines)].T
        level_prev = scale_ref[r, :, whole_prev].T[lines - SUB :]
        level_next = scale_ref[r, :, whole_next].T[:SUB]
        if outer[0] or outer[1]:
            outside = ext_ref[2 * r : 2 * r + 2, samples : samples + blocks]
        if outer[0]:
            level_prev = jnp.where(at_start, placed(outside, SUB - 2), level_prev)
        if outer[1]:
            level_next = jnp.where(at_end, placed(outside, 0), level_next)
        level_ref[r, lines:, :] = jnp.where(row_of < 2, level_next, level_prev)

    def fold(s, buffers):
        even_in, odd_in, edge_in = buffers
        for r in range(REPEATS):
            at = pl.ds(pl.multiple_of(s * SUB, SUB), SUB)
            level = level_ref[r, at, :]
            values = [
                x_ref[r, at, kb * LANES : (kb + 1) * LANES].astype(jnp.float32)
                * level[:, kb : kb + 1]
                for kb in range(blocks)
            ]
            forward = [v.astype(jnp.bfloat16) for v in values]
            turned = [
                jnp.take_along_axis(v, mirror, axis=1, mode="promise_in_bounds") for v in values
            ]
            zero = jnp.zeros((SUB, LANES), jnp.float32)
            backward = []
            for i in range(blocks + 1):
                first = turned[blocks - i] if i > 0 else zero
                rest = turned[blocks - 1 - i] if i < blocks else zero
                backward.append(jnp.where(lane == 0, first, rest).astype(jnp.bfloat16))
            span = blocks // BANDS
            for band in range(BANDS):
                to = slice(band * rows + r * SUB, band * rows + r * SUB + SUB)
                centre = span // 2 + span * band
                for i in range(blocks // 2):
                    ahead = forward[centre + i] if centre + i < blocks else None
                    j = blocks - centre + i
                    behind = backward[j] if j <= blocks else None
                    if behind is None:
                        plus, minus = ahead, ahead
                    elif ahead is None:
                        plus, minus = behind, -behind
                    else:
                        plus, minus = ahead + behind, ahead - behind
                    even_in[to, i * LANES : (i + 1) * LANES] = plus
                    odd_in[to, i * LANES : (i + 1) * LANES] = minus
                far = centre + blocks // 2
                far = far if far < blocks else centre - blocks // 2
                edge_in[to, :] = forward[far].astype(jnp.float32)[:, :1] * sign

    def limits(t):
        return info[2 + 2 * t], info[3 + 2 * t]

    first, last = limits(tile)
    prev_first, prev_last = limits(jnp.maximum(tile - 1, 0))
    next_first, next_last = limits(jnp.minimum(tile + 1, count - 1))
    out_at = 2 + 4 * count
    prev_first = jnp.where(at_start, info[out_at] if outer[0] else 1 << 20, prev_first)
    prev_last = jnp.where(at_start, info[out_at + 1] if outer[0] else -1, prev_last)
    next_first = jnp.where(at_end, info[out_at + 2] if outer[1] else 1 << 20, next_first)
    next_last = jnp.where(at_end, info[out_at + 3] if outer[1] else -1, next_last)

    def shut(values, low, high, at=0):
        out = []
        for n in range(values.shape[1] // LANES):
            inside = jnp.logical_and(low <= at + n, at + n <= high)
            out.append(jnp.where(inside, values[:, n * LANES : (n + 1) * LANES], 0.0))
        return jnp.concatenate(out, axis=1)

    def finish(powers_of):
        ratio, total = None, None
        for band in range(BANDS):
            powers = [powers_of(band, r) for r in range(REPEATS)]
            level = (powers[0] + powers[1]) + (powers[2] + powers[3])
            level = level * (norms[band] / (BANDS * REPEATS))
            total = level if total is None else total + level
            for p, q in zip(powers[:-1], powers[1:]):
                product, both = p * q, p + q
                part = product * lax.rsqrt(product * (both * both))
                ratio = part if ratio is None else ratio + part
        rough = 1.0 - ratio * (2.0 / (BANDS * (REPEATS - 1)))
        return rough, jnp.log(total + 0.05)

    def dots(s, buffers, border):
        even_in, odd_in, edge_in = buffers
        wide = DEPTH // SPLIT
        for part in range(SPLIT):
            columns = slice(part * wide, (part + 1) * wide)
            re = jnp.dot(even_in[...], even_ref[:, columns], preferred_element_type=jnp.float32)
            im = jnp.dot(odd_in[...], odd_ref[:, columns], preferred_element_type=jnp.float32)
            block0 = part * (wide // LANES)
            for g in range(SUB // 8):

                def power(band, r):
                    at = slice(band * rows + r * SUB + g * 8, band * rows + r * SUB + g * 8 + 8)
                    extra = jnp.concatenate([edge_in[at]] * (wide // LANES), axis=1)
                    a, b = re[at] + extra, im[at]
                    return a * a + b * b + 0.05 / norms[band]

                rough, struct = finish(power)
                if border:
                    rough_ref[g * 8 : g * 8 + 8, columns] = shut(rough, prev_first, prev_last, block0)
                    at = SUB + lines + g * 8
                    rough_ref[at : at + 8, columns] = shut(rough, next_first, next_last, block0)
                else:
                    line0 = pl.multiple_of(s * SUB + g * 8, 8)
                    rough_ref[pl.ds(line0 + SUB, 8), columns] = shut(rough, first, last, block0)
                    struct_ref[pl.ds(line0, 8), columns] = struct

    bufs = [scratch[0:3], scratch[3:6]]
    first_copy.wait()
    fold(0, bufs[0])
    for copy in [own] + edges + tables:
        copy.wait()
    for r in range(REPEATS):
        for kb in range(blocks):
            columns = slice(kb * LANES, (kb + 1) * LANES)
            a = near_ref[0, r, :, columns].astype(jnp.float32)
            b = near_ref[1, r, :, columns].astype(jnp.float32)
            if outer[0]:
                a = jnp.where(at_start, placed(ext_ref[2 * r : 2 * r + 2, columns], SUB - 2), a)
            if outer[1]:
                b = jnp.where(at_end, placed(ext_ref[2 * r : 2 * r + 2, columns], 0), b)
            low = lax.broadcasted_iota(jnp.int32, (SUB, LANES), 0) < 2
            x_ref[r, lines:, columns] = jnp.where(low, b, a).astype(jnp.bfloat16)

    if gives_edge:
        give_cols = pl.ds(pl.multiple_of(jnp.where(flip == 1, 0, line_count - lines), lines), lines)
        give_tile = jnp.where(flip == 1, 0, count - 1)
        for r in range(REPEATS):
            at = slice(2 * r, 2 * r + 2)
            for kb in range(blocks):
                columns = slice(kb * LANES, (kb + 1) * LANES)
                piece = near_ref[2, r, :, columns].astype(jnp.float32)
                give_ref[at, columns] = jnp.where(flip == 1, piece[:2], piece[SUB - 2 :])
            level = scale_ref[r, :, give_cols].T
            level = jnp.where(flip == 1, level[:2], level[lines - 2 :])
            edge_first = info[2 + 2 * give_tile].astype(jnp.float32)
            edge_last = info[3 + 2 * give_tile].astype(jnp.float32)
            give_ref[at, samples:] = jnp.concatenate(
                [
                    level,
                    jnp.full((2, 1), edge_first, jnp.float32),
                    jnp.full((2, 1), edge_last, jnp.float32),
                    jnp.zeros((2, LANES - blocks - 2), jnp.float32),
                ],
                axis=1,
            )


    def pair(i, carry):
        dots(2 * i, bufs[0], False)
        fold(2 * i + 1, bufs[1])
        dots(2 * i + 1, bufs[1], False)
        fold(2 * i + 2, bufs[0])
        return carry

    lax.fori_loop(0, parts // 2, pair, 0)
    dots(parts, bufs[0], True)

    pick = info[2 + 2 * count + tile]
    chosen = struct_ref[:, pl.ds(pl.multiple_of(pick * LANES, LANES), LANES)]
    score = jnp.sum(chosen) * (1.0 / (LANES * lines)) + values[2 + 3 * count + tile]
    smooth = TAPS[0] * rough_ref[SUB - 2 : SUB - 2 + lines, :]
    for k in range(1, 5):
        smooth = smooth + TAPS[k] * rough_ref[SUB - 2 + k : SUB - 2 + k + lines, :]
    maps = (smooth, shut(struct_ref[...], first, last))
    half = (send_ref.shape[0] - 8) // 2
    strip = DEPTH // strips
    low = info[1] % 2 == 0
    for m, whole in enumerate(maps):
        for zb in range(DEPTH // LANES):
            block = whole[:, zb * LANES : (zb + 1) * LANES].T
            for s in range(LANES // (2 * strip)):
                a = block[2 * s * strip : (2 * s + 1) * strip]
                b = block[(2 * s + 1) * strip : (2 * s + 2) * strip]
                at = m * half + zb * (LANES // 2) + s * strip
                keep_ref[at : at + strip, :] = jnp.where(low, a, b)
                send_ref[at : at + strip, :] = jnp.where(low, b, a)
    row = jnp.full((8, lines), score, jnp.float32)
    keep_ref[2 * half :, :] = row
    send_ref[2 * half :, :] = row


SUB = 16
MIB = 1024 * 1024
NEAR = (True, True, True)
LIMIT = (48 * MIB, 48 * MIB, 48 * MIB)
SPLIT = 2


def maps_call(step, count, outer, gives_edge, info, spectra, scales, extra, table, norms, edge, strips):
    samples = spectra.shape[-1]
    rows = BANDS * REPEATS * SUB
    out = jax.ShapeDtypeStruct((DEPTH + 8, LANES), jnp.float32)
    half = samples // 2
    whole = pl.BlockSpec(memory_space=pltpu.VMEM)
    remote = pl.BlockSpec(memory_space=pltpu.HBM)
    scales = jnp.swapaxes(scales, 1, 2)
    has_ext = outer[0] or outer[1]
    waits = len(extra) > has_ext
    outs = [out, out]
    if gives_edge:
        outs.append(jax.ShapeDtypeStruct((2 * REPEATS, samples + LANES), jnp.float32))
    pair = [
        pltpu.VMEM((rows, half), jnp.bfloat16),
        pltpu.VMEM((rows, half), jnp.bfloat16),
        pltpu.VMEM((rows, LANES), jnp.float32),
    ]
    scratch = [
        pltpu.VMEM((LANES + 2 * SUB, DEPTH), jnp.float32),
        pltpu.VMEM((LANES, DEPTH), jnp.float32),
        pltpu.VMEM((REPEATS, LANES + SUB, samples), jnp.bfloat16),
        pltpu.VMEM((REPEATS, LANES + SUB, samples // LANES), jnp.float32),
        pltpu.VMEM((3, REPEATS, SUB, samples), jnp.bfloat16),
        pltpu.SemaphoreType.DMA((7,)),
    ] + pair + pair
    near_tables = NEAR[step]
    if not near_tables:
        scratch.append(pltpu.VMEM((2, half, DEPTH), jnp.bfloat16))
    return pl.pallas_call(
        functools.partial(
            maps_kernel, norms, edge, strips, step, count, outer, gives_edge, waits, near_tables
        ),
        in_specs=[pl.BlockSpec(memory_space=pltpu.SMEM)]
        + [remote, whole, whole if near_tables else remote]
        + [whole] * has_ext + [pl.BlockSpec(memory_space=pl.ANY)] * waits,
        out_specs=[whole] * len(outs),
        scratch_shapes=scratch,
        out_shape=outs,
        compiler_params=pltpu.CompilerParams(vmem_limit_bytes=LIMIT[step]),
        cost_estimate=pl.CostEstimate(
            flops=5 * BANDS * REPEATS * (LANES + SUB) * samples * DEPTH,
            bytes_accessed=2 * REPEATS * LANES * samples + 4 * samples * DEPTH,
            transcendentals=0,
        ),
        name="maps",
    )(info, spectra, scales, table, *extra)


def merge_kernel(rows, strip, shares, tied, vol, keep_ref, recv_ref, *outs):
    outs = outs[len(outs) - shares - tied : len(outs) - tied]
    top_a, top_b = keep_ref[2 * rows : 2 * rows + 8], recv_ref[2 * rows : 2 * rows + 8]
    top = jnp.maximum(top_a, top_b)
    wa, wb = jnp.exp(top_a - top), jnp.exp(top_b - top)
    row = lax.broadcasted_iota(jnp.int32, (8, LANES), 0)
    tail = jnp.where(row < 4, top, wa + wb)
    wa, wb = wa[:1], wb[:1]
    mine = vol[0] // 2
    for d in range(shares):
        t = jnp.bitwise_xor(mine, d)
        at = pl.ds(pl.multiple_of(t * strip, strip), strip)
        struct = pl.ds(pl.multiple_of(rows + t * strip, strip), strip)
        sa, sb = keep_ref[at, :], recv_ref[at, :]
        first, other = wa * sa, wb * sb
        outs[d][:strip] = first + other
        outs[d][strip : 2 * strip] = first * sa + other * sb
        outs[d][2 * strip : 3 * strip] = wa * keep_ref[struct, :] + wb * recv_ref[struct, :]
        outs[d][3 * strip :] = tail


def merge_call(vol, keep, recv, later, strips):
    strip, shares = DEPTH // strips, strips // 2
    whole = pl.BlockSpec(memory_space=pltpu.VMEM)
    remote = pl.BlockSpec(memory_space=pl.ANY)
    out = jax.ShapeDtypeStruct((3 * strip + 8, LANES), jnp.float32)
    tied = [jax.ShapeDtypeStruct(a.shape, a.dtype) for a in later[:1]]
    return pl.pallas_call(
        functools.partial(merge_kernel, DEPTH // 2, strip, shares, len(tied)),
        in_specs=[pl.BlockSpec(memory_space=pltpu.SMEM), whole, whole] + [remote] * len(later),
        out_specs=[whole] * shares + [remote] * len(tied),
        out_shape=[out] * shares + tied,
        input_output_aliases={3: shares} if tied else {},
        compiler_params=pltpu.CompilerParams(vmem_limit_bytes=4 * 1024 * 1024),
        name="merge",
    )(vol, keep, recv, *later)


def final_kernel(strip, count, shares, info, *refs):
    parts, (angio_ref, joined_ref, spread_ref) = refs[: count * shares], refs[count * shares :]
    for i in range(count):
        mine = parts[i * shares : (i + 1) * shares]
        tops = [p[3 * strip : 3 * strip + 1] for p in mine]
        top = functools.reduce(jnp.maximum, tops)
        scales = [jnp.exp(t - top) for t in tops]
        weight = functools.reduce(
            lambda a, b: a + b, [w * p[3 * strip + 4 : 3 * strip + 5] for w, p in zip(scales, mine)]
        )
        scales = [w / weight for w in scales]
        mean, second, joined = (
            functools.reduce(
                lambda a, b: a + b,
                [w * p[m * strip : (m + 1) * strip] for w, p in zip(scales, mine)],
            )
            for m in range(3)
        )
        tile = jnp.where(info[0] == 1, count - 1 - i, i)
        columns = pl.ds(pl.multiple_of(tile * LANES, LANES), LANES)
        angio_ref[:, columns] = mean
        joined_ref[:, columns] = joined
        spread_ref[:, columns] = jnp.sqrt(second - mean * mean + 0.01)


def final_call(info, parts, count, strips):
    strip, shares = DEPTH // strips, strips // 2
    whole = pl.BlockSpec(memory_space=pltpu.VMEM)
    out = jax.ShapeDtypeStruct((strip, count * LANES), jnp.float32)
    return pl.pallas_call(
        functools.partial(final_kernel, strip, count, shares),
        in_specs=[pl.BlockSpec(memory_space=pltpu.SMEM)] + [whole] * len(parts),
        out_specs=[whole] * 3,
        out_shape=[out] * 3,
        compiler_params=pltpu.CompilerParams(vmem_limit_bytes=4 * 1024 * 1024),
        name="final",
    )(info, *parts)


def edge_rows(spectra, scales, start, block):
    lines = lax.dynamic_slice_in_dim(spectra, start, 2, axis=1).astype(jnp.float32)
    level = lax.dynamic_slice_in_dim(scales, start, 2, axis=1)
    rows = lines.shape[0] * 2
    limits = jnp.broadcast_to(block.astype(jnp.float32)[None], (rows, 2))
    rest = jnp.zeros((rows, LANES - level.shape[2] - 2), jnp.float32)
    return jnp.concatenate(
        [lines.reshape(rows, -1), level.reshape(rows, -1), limits, rest], axis=1
    )


def on_device(tiles, strips, spectra, scales, retina, quality, bias):
    spectra, scales, quality, bias = spectra[0], scales[0], quality[0], bias[0]
    samples = spectra.shape[-1]
    count = retina.shape[0]
    table, norms, edge = constants(samples)
    table = jnp.asarray(table)
    here = lax.axis_index("tile")
    vol = lax.axis_index("vol")
    lines = spectra.shape[1]

    at = samples + scales.shape[2]
    none = jnp.array([1 << 20, -1], jnp.float32)
    flip = (here == 1).astype(jnp.int32) if tiles == 2 else jnp.zeros((), jnp.int32)
    info = jnp.concatenate(
        [
            flip[None].astype(jnp.float32),
            vol[None].astype(jnp.float32),
            retina.reshape(-1).astype(jnp.float32),
            quality.astype(jnp.float32),
            bias,
        ]
    )

    def with_limits(before, after):
        before_block = jnp.where(here == 0, none, before[0, at : at + 2])
        after_block = jnp.where(here == tiles - 1, none, after[0, at : at + 2])
        return jnp.concatenate([info, before_block, after_block])

    if tiles == 2:
        outside = [(False, False)] * (count - 1) + [(True, True)]
    else:
        up = [(i, i + 1) for i in range(tiles - 1)]
        down = [(i + 1, i) for i in range(tiles - 1)]
        before = lax.ppermute(edge_rows(spectra, scales, lines - 2, retina[count - 1]), "tile", up)
        after = lax.ppermute(edge_rows(spectra, scales, 0, retina[0]), "tile", down)
        info = with_limits(before, after)
        outside = [(i == 0, i == count - 1) for i in range(count)]

    shares = strips // 2
    swap = [(v, v ^ 1) for v in range(strips)]
    kept, arrived, parts = [], [], []

    def merge(i, later):
        outs = merge_call(vol[None], kept[i], arrived[i], later, strips)
        got = [
            lax.ppermute(p, "vol", [(v, v ^ (2 * d)) for v in range(strips)])
            for d, p in zip(range(1, shares), outs[1:])
        ]
        parts.append([outs[0]] + got)
        return outs[-1]

    for i in range(count):
        outer = outside[i]
        gives_edge = tiles == 2 and i == 0
        extra = []
        if outer[0] or outer[1]:
            if tiles == 2:
                after = lax.ppermute(given, "tile", [(0, 1), (1, 0)])
                step_info = with_limits(after, after)
            else:
                step_info = info
            extra.append(after if outer[1] else before)
        else:
            step_info = info
        if i >= 2:
            if i == 2:
                merge(0, [])
            extra.append(parts[i - 2][0])
        send, keep, *rest = maps_call(
            i, count, outer, gives_edge, step_info,
            spectra, scales, extra, table, norms, edge, strips,
        )
        if gives_edge:
            given = rest[0]
        kept.append(keep)
        if i >= 2:
            send = merge(i - 1, [send] + parts[i - 2][1:])
        arrived.append(lax.ppermute(send, "vol", swap))
    for i in range(len(parts), count):
        merge(i, [])
    flat = [p for own in parts for p in own]
    return tuple(final_call(info, flat, count, strips))


def solution(mesh):
    return jax.shard_map(
        functools.partial(on_device, mesh.shape["tile"], mesh.shape["vol"]),
        mesh=mesh,
        in_specs=(
            P(("study", "vol"), None, "tile", None),
            P(("study", "vol"), None, "tile", None),
            P(("study", "tile"), None),
            P(("study", "vol"), "tile"),
            P(("study", "vol"), "tile"),
        ),
        out_specs=(P(("study", "vol"), "tile"),) * 3,
        check_vma=False,
    )
```

```python
import functools
import math

import jax
import jax.numpy as jnp
import ml_dtypes
import numpy as np
from jax import lax
from jax.experimental import pallas as pl
from jax.experimental.pallas import tpu as pltpu
from jax.sharding import PartitionSpec as P

DEPTH = 512
BANDS = 4
REPEATS = 4
LANES = 128
HALO = 8
TAPS = (1.0 / 9.0, 2.0 / 9.0, 3.0 / 9.0, 2.0 / 9.0, 1.0 / 9.0)


def constants(samples):
    half = samples // 2
    distance = np.arange(half, dtype=np.float64)
    gauss = np.exp(-0.5 * (distance / (samples / 8)) ** 2)
    turn = 2.0 * np.pi * ((np.arange(half)[:, None] * np.arange(DEPTH)[None, :]) % samples) / samples
    even = gauss[:, None] * np.cos(turn)
    even[0] *= 0.5
    odd = gauss[:, None] * np.sin(turn)
    norms = []
    for band in range(BANDS):
        away = np.arange(samples) - (band + 0.5) * samples / BANDS
        window = np.where(np.abs(away) <= half, np.exp(-0.5 * (away / (samples / 8)) ** 2), 0.0)
        norms.append(float(1.0 / np.sum(window * window)))
    edge = float(np.exp(-0.5 * (half / (samples / 8)) ** 2))
    return np.stack([even, odd]).astype(ml_dtypes.bfloat16), norms, edge


class Whole:
    def __init__(self, ref):
        self.ref = ref

    def __getitem__(self, at):
        return self.ref[at].astype(jnp.int32)


def maps_kernel(
    norms, edge, strips, step, count, outer, gives_edge, waits, near_tables, values, x_hbm, scale_ref,
    table_in, *refs,
):
    refs = list(refs)
    ext_ref = refs.pop(0) if outer[0] or outer[1] else None
    if waits:
        refs.pop(0)
    send_ref, keep_ref = refs.pop(0), refs.pop(0)
    give_ref = refs.pop(0) if gives_edge else None
    rough_ref, struct_ref, x_ref, level_ref, near_ref, sems = refs[:6]
    scratch = refs[6:]
    if not near_tables:
        table_ref = scratch.pop()
    lines = LANES
    samples = x_hbm.shape[-1]
    blocks = samples // LANES
    parts = lines // SUB
    rows = REPEATS * SUB
    info = Whole(values)
    flip = info[0]
    tile = jnp.where(flip == 1, count - 1 - step, step)
    lane = lax.broadcasted_iota(jnp.int32, (SUB, LANES), 1)
    mirror = jnp.where(lane == 0, 0, LANES - lane)
    sign = jnp.where(lane % 2 == 0, edge, -edge)

    line_count = x_hbm.shape[1]
    base = pl.multiple_of(tile * lines, lines)
    base_prev = pl.multiple_of(jnp.maximum(base - SUB, 0), SUB)
    base_next = pl.multiple_of(jnp.minimum(base + lines, line_count - SUB), SUB)
    first_copy = pltpu.make_async_copy(
        x_hbm.at[:, pl.ds(base, SUB), :], x_ref.at[:, :SUB, :], sems.at[0]
    )
    own = pltpu.make_async_copy(
        x_hbm.at[:, pl.ds(pl.multiple_of(base + SUB, SUB), lines - SUB), :],
        x_ref.at[:, SUB:lines, :],
        sems.at[5],
    )
    tables = []
    if near_tables:
        even_ref, odd_ref = table_in.at[0], table_in.at[1]
    else:
        even_ref, odd_ref = table_ref.at[0], table_ref.at[1]
        tables.append(pltpu.make_async_copy(table_in, table_ref, sems.at[1]))
    starts = [base_prev, base_next]
    if gives_edge:
        base_give = pl.multiple_of(jnp.where(flip == 1, 0, line_count - SUB), SUB)
        starts.append(base_give)
    edges = [
        pltpu.make_async_copy(x_hbm.at[:, pl.ds(start, SUB), :], near_ref.at[n], sems.at[(3, 4, 6)[n]])
        for n, start in enumerate(starts)
    ]
    for copy in [first_copy] + tables + edges + [own]:
        copy.start()

    at_start, at_end = tile == 0, tile == count - 1
    whole_prev = pl.ds(pl.multiple_of(jnp.maximum(base - lines, 0), lines), lines)
    whole_next = pl.ds(pl.multiple_of(jnp.minimum(base + lines, line_count - lines), lines), lines)

    def placed(values, at):
        above = jnp.zeros((at, values.shape[1]), values.dtype)
        below = jnp.zeros((SUB - 2 - at, values.shape[1]), values.dtype)
        return jnp.concatenate([piece for piece in (above, values, below) if piece.shape[0]], axis=0)

    row_of = lax.broadcasted_iota(jnp.int32, (SUB, blocks), 0)
    for r in range(REPEATS):
        level_ref[r, :lines, :] = scale_ref[r, :, pl.ds(base, lines)].T
        level_prev = scale_ref[r, :, whole_prev].T[lines - SUB :]
        level_next = scale_ref[r, :, whole_next].T[:SUB]
        if outer[0] or outer[1]:
            outside = ext_ref[2 * r : 2 * r + 2, samples : samples + blocks]
        if outer[0]:
            level_prev = jnp.where(at_start, placed(outside, SUB - 2), level_prev)
        if outer[1]:
            level_next = jnp.where(at_end, placed(outside, 0), level_next)
        level_ref[r, lines:, :] = jnp.where(row_of < 2, level_next, level_prev)

    def fold(s, buffers):
        even_in, odd_in, edge_in = buffers
        for r in range(REPEATS):
            at = pl.ds(pl.multiple_of(s * SUB, SUB), SUB)
            level = level_ref[r, at, :]
            values = [
                x_ref[r, at, kb * LANES : (kb + 1) * LANES].astype(jnp.float32)
                * level[:, kb : kb + 1]
                for kb in range(blocks)
            ]
            forward = [v.astype(jnp.bfloat16) for v in values]
            turned = [
                jnp.take_along_axis(v, mirror, axis=1, mode="promise_in_bounds") for v in values
            ]
            zero = jnp.zeros((SUB, LANES), jnp.float32)
            backward = []
            for i in range(blocks + 1):
                first = turned[blocks - i] if i > 0 else zero
                rest = turned[blocks - 1 - i] if i < blocks else zero
                backward.append(jnp.where(lane == 0, first, rest).astype(jnp.bfloat16))
            span = blocks // BANDS
            for band in range(BANDS):
                to = slice(band * rows + r * SUB, band * rows + r * SUB + SUB)
                centre = span // 2 + span * band
                for i in range(blocks // 2):
                    ahead = forward[centre + i] if centre + i < blocks else None
                    j = blocks - centre + i
                    behind = backward[j] if j <= blocks else None
                    if behind is None:
                        plus, minus = ahead, ahead
                    elif ahead is None:
                        plus, minus = behind, -behind
                    else:
                        plus, minus = ahead + behind, ahead - behind
                    even_in[to, i * LANES : (i + 1) * LANES] = plus
                    odd_in[to, i * LANES : (i + 1) * LANES] = minus
                far = centre + blocks // 2
                far = far if far < blocks else centre - blocks // 2
                edge_in[to, :] = forward[far].astype(jnp.float32)[:, :1] * sign

    def limits(t):
        return info[2 + 2 * t], info[3 + 2 * t]

    first, last = limits(tile)
    prev_first, prev_last = limits(jnp.maximum(tile - 1, 0))
    next_first, next_last = limits(jnp.minimum(tile + 1, count - 1))
    out_at = 2 + 4 * count
    prev_first = jnp.where(at_start, info[out_at] if outer[0] else 1 << 20, prev_first)
    prev_last = jnp.where(at_start, info[out_at + 1] if outer[0] else -1, prev_last)
    next_first = jnp.where(at_end, info[out_at + 2] if outer[1] else 1 << 20, next_first)
    next_last = jnp.where(at_end, info[out_at + 3] if outer[1] else -1, next_last)

    def shut(values, low, high, at=0):
        out = []
        for n in range(values.shape[1] // LANES):
            inside = jnp.logical_and(low <= at + n, at + n <= high)
            out.append(jnp.where(inside, values[:, n * LANES : (n + 1) * LANES], 0.0))
        return jnp.concatenate(out, axis=1)

    def finish(powers_of):
        ratio, total = None, None
        for band in range(BANDS):
            powers = [powers_of(band, r) for r in range(REPEATS)]
            level = (powers[0] + powers[1]) + (powers[2] + powers[3])
            level = level * (norms[band] / (BANDS * REPEATS))
            total = level if total is None else total + level
            for p, q in zip(powers[:-1], powers[1:]):
                product, both = p * q, p + q
                part = product * lax.rsqrt(product * (both * both))
                ratio = part if ratio is None else ratio + part
        rough = 1.0 - ratio * (2.0 / (BANDS * (REPEATS - 1)))
        return rough, jnp.log(total + 0.05)

    def dots(s, buffers, border):
        even_in, odd_in, edge_in = buffers
        wide = DEPTH // SPLIT

        def product(part, source, table):
            columns = slice(part * wide, (part + 1) * wide)
            return jnp.dot(source[...], table[:, columns], preferred_element_type=jnp.float32)

        def complete(part, re, im):
            columns = slice(part * wide, (part + 1) * wide)
            block0 = part * (wide // LANES)
            for g in range(SUB // 8):

                def power(band, r):
                    at = slice(band * rows + r * SUB + g * 8, band * rows + r * SUB + g * 8 + 8)
                    extra = jnp.concatenate([edge_in[at]] * (wide // LANES), axis=1)
                    a, b = re[at] + extra, im[at]
                    return a * a + b * b + 0.05 / norms[band]

                rough, struct = finish(power)
                if border:
                    rough_ref[g * 8 : g * 8 + 8, columns] = shut(rough, prev_first, prev_last, block0)
                    at = SUB + lines + g * 8
                    rough_ref[at : at + 8, columns] = shut(rough, next_first, next_last, block0)
                else:
                    line0 = pl.multiple_of(s * SUB + g * 8, 8)
                    rough_ref[pl.ds(line0 + SUB, 8), columns] = shut(rough, first, last, block0)
                    struct_ref[pl.ds(line0, 8), columns] = struct

        re0 = product(0, even_in, even_ref)
        im0 = product(0, odd_in, odd_ref)
        re1 = product(1, even_in, even_ref)
        complete(0, re0, im0)
        im1 = product(1, odd_in, odd_ref)
        complete(1, re1, im1)

    bufs = [scratch[0:3], scratch[3:6]]
    first_copy.wait()
    fold(0, bufs[0])
    for copy in [own] + edges + tables:
        copy.wait()
    for r in range(REPEATS):
        for kb in range(blocks):
            columns = slice(kb * LANES, (kb + 1) * LANES)
            a = near_ref[0, r, :, columns].astype(jnp.float32)
            b = near_ref[1, r, :, columns].astype(jnp.float32)
            if outer[0]:
                a = jnp.where(at_start, placed(ext_ref[2 * r : 2 * r + 2, columns], SUB - 2), a)
            if outer[1]:
                b = jnp.where(at_end, placed(ext_ref[2 * r : 2 * r + 2, columns], 0), b)
            low = lax.broadcasted_iota(jnp.int32, (SUB, LANES), 0) < 2
            x_ref[r, lines:, columns] = jnp.where(low, b, a).astype(jnp.bfloat16)

    if gives_edge:
        give_cols = pl.ds(pl.multiple_of(jnp.where(flip == 1, 0, line_count - lines), lines), lines)
        give_tile = jnp.where(flip == 1, 0, count - 1)
        for r in range(REPEATS):
            at = slice(2 * r, 2 * r + 2)
            for kb in range(blocks):
                columns = slice(kb * LANES, (kb + 1) * LANES)
                piece = near_ref[2, r, :, columns].astype(jnp.float32)
                give_ref[at, columns] = jnp.where(flip == 1, piece[:2], piece[SUB - 2 :])
            level = scale_ref[r, :, give_cols].T
            level = jnp.where(flip == 1, level[:2], level[lines - 2 :])
            edge_first = info[2 + 2 * give_tile].astype(jnp.float32)
            edge_last = info[3 + 2 * give_tile].astype(jnp.float32)
            give_ref[at, samples:] = jnp.concatenate(
                [
                    level,
                    jnp.full((2, 1), edge_first, jnp.float32),
                    jnp.full((2, 1), edge_last, jnp.float32),
                    jnp.zeros((2, LANES - blocks - 2), jnp.float32),
                ],
                axis=1,
            )


    def pair(i, carry):
        dots(2 * i, bufs[0], False)
        fold(2 * i + 1, bufs[1])
        dots(2 * i + 1, bufs[1], False)
        fold(2 * i + 2, bufs[0])
        return carry

    lax.fori_loop(0, parts // 2, pair, 0)
    dots(parts, bufs[0], True)

    pick = info[2 + 2 * count + tile]
    chosen = struct_ref[:, pl.ds(pl.multiple_of(pick * LANES, LANES), LANES)]
    score = jnp.sum(chosen) * (1.0 / (LANES * lines)) + values[2 + 3 * count + tile]
    smooth = TAPS[0] * rough_ref[SUB - 2 : SUB - 2 + lines, :]
    for k in range(1, 5):
        smooth = smooth + TAPS[k] * rough_ref[SUB - 2 + k : SUB - 2 + k + lines, :]
    maps = (smooth, shut(struct_ref[...], first, last))
    half = (send_ref.shape[0] - 8) // 2
    strip = DEPTH // strips
    low = info[1] % 2 == 0
    for m, whole in enumerate(maps):
        for zb in range(DEPTH // LANES):
            block = whole[:, zb * LANES : (zb + 1) * LANES].T
            for s in range(LANES // (2 * strip)):
                a = block[2 * s * strip : (2 * s + 1) * strip]
                b = block[(2 * s + 1) * strip : (2 * s + 2) * strip]
                at = m * half + zb * (LANES // 2) + s * strip
                keep_ref[at : at + strip, :] = jnp.where(low, a, b)
                send_ref[at : at + strip, :] = jnp.where(low, b, a)
    row = jnp.full((8, lines), score, jnp.float32)
    keep_ref[2 * half :, :] = row
    send_ref[2 * half :, :] = row


SUB = 16
MIB = 1024 * 1024
NEAR = (True, True, True)
LIMIT = (48 * MIB, 48 * MIB, 48 * MIB)
SPLIT = 2


def maps_call(step, count, outer, gives_edge, info, spectra, scales, extra, table, norms, edge, strips):
    samples = spectra.shape[-1]
    rows = BANDS * REPEATS * SUB
    out = jax.ShapeDtypeStruct((DEPTH + 8, LANES), jnp.float32)
    half = samples // 2
    whole = pl.BlockSpec(memory_space=pltpu.VMEM)
    remote = pl.BlockSpec(memory_space=pltpu.HBM)
    scales = jnp.swapaxes(scales, 1, 2)
    has_ext = outer[0] or outer[1]
    waits = len(extra) > has_ext
    outs = [out, out]
    if gives_edge:
        outs.append(jax.ShapeDtypeStruct((2 * REPEATS, samples + LANES), jnp.float32))
    pair = [
        pltpu.VMEM((rows, half), jnp.bfloat16),
        pltpu.VMEM((rows, half), jnp.bfloat16),
        pltpu.VMEM((rows, LANES), jnp.float32),
    ]
    scratch = [
        pltpu.VMEM((LANES + 2 * SUB, DEPTH), jnp.float32),
        pltpu.VMEM((LANES, DEPTH), jnp.float32),
        pltpu.VMEM((REPEATS, LANES + SUB, samples), jnp.bfloat16),
        pltpu.VMEM((REPEATS, LANES + SUB, samples // LANES), jnp.float32),
        pltpu.VMEM((3, REPEATS, SUB, samples), jnp.bfloat16),
        pltpu.SemaphoreType.DMA((7,)),
    ] + pair + pair
    near_tables = NEAR[step]
    if not near_tables:
        scratch.append(pltpu.VMEM((2, half, DEPTH), jnp.bfloat16))
    return pl.pallas_call(
        functools.partial(
            maps_kernel, norms, edge, strips, step, count, outer, gives_edge, waits, near_tables
        ),
        in_specs=[pl.BlockSpec(memory_space=pltpu.SMEM)]
        + [remote, whole, whole if near_tables else remote]
        + [whole] * has_ext + [pl.BlockSpec(memory_space=pl.ANY)] * waits,
        out_specs=[whole] * len(outs),
        scratch_shapes=scratch,
        out_shape=outs,
        compiler_params=pltpu.CompilerParams(vmem_limit_bytes=LIMIT[step]),
        cost_estimate=pl.CostEstimate(
            flops=5 * BANDS * REPEATS * (LANES + SUB) * samples * DEPTH,
            bytes_accessed=2 * REPEATS * LANES * samples + 4 * samples * DEPTH,
            transcendentals=0,
        ),
        name="maps",
    )(info, spectra, scales, table, *extra)


def merge_kernel(rows, strip, shares, tied, vol, keep_ref, recv_ref, *outs):
    outs = outs[len(outs) - shares - tied : len(outs) - tied]
    top_a, top_b = keep_ref[2 * rows : 2 * rows + 8], recv_ref[2 * rows : 2 * rows + 8]
    top = jnp.maximum(top_a, top_b)
    wa, wb = jnp.exp(top_a - top), jnp.exp(top_b - top)
    row = lax.broadcasted_iota(jnp.int32, (8, LANES), 0)
    tail = jnp.where(row < 4, top, wa + wb)
    wa, wb = wa[:1], wb[:1]
    mine = vol[0] // 2
    for d in range(shares):
        t = jnp.bitwise_xor(mine, d)
        at = pl.ds(pl.multiple_of(t * strip, strip), strip)
        struct = pl.ds(pl.multiple_of(rows + t * strip, strip), strip)
        sa, sb = keep_ref[at, :], recv_ref[at, :]
        first, other = wa * sa, wb * sb
        outs[d][:strip] = first + other
        outs[d][strip : 2 * strip] = first * sa + other * sb
        outs[d][2 * strip : 3 * strip] = wa * keep_ref[struct, :] + wb * recv_ref[struct, :]
        outs[d][3 * strip :] = tail


def merge_call(vol, keep, recv, later, strips):
    strip, shares = DEPTH // strips, strips // 2
    whole = pl.BlockSpec(memory_space=pltpu.VMEM)
    remote = pl.BlockSpec(memory_space=pl.ANY)
    out = jax.ShapeDtypeStruct((3 * strip + 8, LANES), jnp.float32)
    tied = [jax.ShapeDtypeStruct(a.shape, a.dtype) for a in later[:1]]
    return pl.pallas_call(
        functools.partial(merge_kernel, DEPTH // 2, strip, shares, len(tied)),
        in_specs=[pl.BlockSpec(memory_space=pltpu.SMEM), whole, whole] + [remote] * len(later),
        out_specs=[whole] * shares + [remote] * len(tied),
        out_shape=[out] * shares + tied,
        input_output_aliases={3: shares} if tied else {},
        compiler_params=pltpu.CompilerParams(vmem_limit_bytes=4 * 1024 * 1024),
        name="merge",
    )(vol, keep, recv, *later)


def final_kernel(strip, count, shares, info, *refs):
    parts, (angio_ref, joined_ref, spread_ref) = refs[: count * shares], refs[count * shares :]
    for i in range(count):
        mine = parts[i * shares : (i + 1) * shares]
        tops = [p[3 * strip : 3 * strip + 1] for p in mine]
        top = functools.reduce(jnp.maximum, tops)
        scales = [jnp.exp(t - top) for t in tops]
        weight = functools.reduce(
            lambda a, b: a + b, [w * p[3 * strip + 4 : 3 * strip + 5] for w, p in zip(scales, mine)]
        )
        scales = [w / weight for w in scales]
        mean, second, joined = (
            functools.reduce(
                lambda a, b: a + b,
                [w * p[m * strip : (m + 1) * strip] for w, p in zip(scales, mine)],
            )
            for m in range(3)
        )
        tile = jnp.where(info[0] == 1, count - 1 - i, i)
        columns = pl.ds(pl.multiple_of(tile * LANES, LANES), LANES)
        angio_ref[:, columns] = mean
        joined_ref[:, columns] = joined
        spread_ref[:, columns] = jnp.sqrt(second - mean * mean + 0.01)


def final_call(info, parts, count, strips):
    strip, shares = DEPTH // strips, strips // 2
    whole = pl.BlockSpec(memory_space=pltpu.VMEM)
    out = jax.ShapeDtypeStruct((strip, count * LANES), jnp.float32)
    return pl.pallas_call(
        functools.partial(final_kernel, strip, count, shares),
        in_specs=[pl.BlockSpec(memory_space=pltpu.SMEM)] + [whole] * len(parts),
        out_specs=[whole] * 3,
        out_shape=[out] * 3,
        compiler_params=pltpu.CompilerParams(vmem_limit_bytes=4 * 1024 * 1024),
        name="final",
    )(info, *parts)


def edge_rows(spectra, scales, start, block):
    lines = lax.dynamic_slice_in_dim(spectra, start, 2, axis=1).astype(jnp.float32)
    level = lax.dynamic_slice_in_dim(scales, start, 2, axis=1)
    rows = lines.shape[0] * 2
    limits = jnp.broadcast_to(block.astype(jnp.float32)[None], (rows, 2))
    rest = jnp.zeros((rows, LANES - level.shape[2] - 2), jnp.float32)
    return jnp.concatenate(
        [lines.reshape(rows, -1), level.reshape(rows, -1), limits, rest], axis=1
    )


def on_device(tiles, strips, spectra, scales, retina, quality, bias):
    spectra, scales, quality, bias = spectra[0], scales[0], quality[0], bias[0]
    samples = spectra.shape[-1]
    count = retina.shape[0]
    table, norms, edge = constants(samples)
    table = jnp.asarray(table)
    here = lax.axis_index("tile")
    vol = lax.axis_index("vol")
    lines = spectra.shape[1]

    at = samples + scales.shape[2]
    none = jnp.array([1 << 20, -1], jnp.float32)
    flip = (here == 1).astype(jnp.int32) if tiles == 2 else jnp.zeros((), jnp.int32)
    info = jnp.concatenate(
        [
            flip[None].astype(jnp.float32),
            vol[None].astype(jnp.float32),
            retina.reshape(-1).astype(jnp.float32),
            quality.astype(jnp.float32),
            bias,
        ]
    )

    def with_limits(before, after):
        before_block = jnp.where(here == 0, none, before[0, at : at + 2])
        after_block = jnp.where(here == tiles - 1, none, after[0, at : at + 2])
        return jnp.concatenate([info, before_block, after_block])

    if tiles == 2:
        outside = [(False, False)] * (count - 1) + [(True, True)]
    else:
        up = [(i, i + 1) for i in range(tiles - 1)]
        down = [(i + 1, i) for i in range(tiles - 1)]
        before = lax.ppermute(edge_rows(spectra, scales, lines - 2, retina[count - 1]), "tile", up)
        after = lax.ppermute(edge_rows(spectra, scales, 0, retina[0]), "tile", down)
        info = with_limits(before, after)
        outside = [(i == 0, i == count - 1) for i in range(count)]

    shares = strips // 2
    swap = [(v, v ^ 1) for v in range(strips)]
    kept, arrived, parts = [], [], []

    def merge(i, later):
        outs = merge_call(vol[None], kept[i], arrived[i], later, strips)
        got = [
            lax.ppermute(outs[d], "vol", [(v, v ^ (2 * d)) for v in range(strips)])
            for d in [*range(2, shares), 1][: shares - 1]
        ]
        parts.append([outs[0]] + got)
        return outs[-1]

    for i in range(count):
        outer = outside[i]
        gives_edge = tiles == 2 and i == 0
        extra = []
        if outer[0] or outer[1]:
            if tiles == 2:
                after = lax.ppermute(given, "tile", [(0, 1), (1, 0)])
                step_info = with_limits(after, after)
            else:
                step_info = info
            extra.append(after if outer[1] else before)
        else:
            step_info = info
        if i >= 2:
            if i == 2:
                merge(0, [])
            extra.append(parts[i - 2][0])
        send, keep, *rest = maps_call(
            i, count, outer, gives_edge, step_info,
            spectra, scales, extra, table, norms, edge, strips,
        )
        if gives_edge:
            given = rest[0]
        kept.append(keep)
        if i >= 2:
            send = merge(i - 1, [send] + parts[i - 2][1:])
        arrived.append(lax.ppermute(send, "vol", swap))
    for i in range(len(parts), count):
        merge(i, [])
    flat = [p for own in parts for p in own]
    return tuple(final_call(info, flat, count, strips))


def solution(mesh):
    return jax.shard_map(
        functools.partial(on_device, mesh.shape["tile"], mesh.shape["vol"]),
        mesh=mesh,
        in_specs=(
            P(("study", "vol"), None, "tile", None),
            P(("study", "vol"), None, "tile", None),
            P(("study", "tile"), None),
            P(("study", "vol"), "tile"),
            P(("study", "vol"), "tile"),
        ),
        out_specs=(P(("study", "vol"), "tile"),) * 3,
        check_vma=False,
    )
```

```python
import functools
import math

import jax
import jax.numpy as jnp
import ml_dtypes
import numpy as np
from jax import lax
from jax.experimental import pallas as pl
from jax.experimental.pallas import tpu as pltpu
from jax.sharding import PartitionSpec as P

DEPTH = 512
BANDS = 4
REPEATS = 4
LANES = 128
HALO = 8
TAPS = (1.0 / 9.0, 2.0 / 9.0, 3.0 / 9.0, 2.0 / 9.0, 1.0 / 9.0)


def constants(samples):
    half = samples // 2
    distance = np.arange(half, dtype=np.float64)
    gauss = np.exp(-0.5 * (distance / (samples / 8)) ** 2)
    turn = 2.0 * np.pi * ((np.arange(half)[:, None] * np.arange(DEPTH)[None, :]) % samples) / samples
    even = gauss[:, None] * np.cos(turn)
    even[0] *= 0.5
    odd = gauss[:, None] * np.sin(turn)
    norms = []
    for band in range(BANDS):
        away = np.arange(samples) - (band + 0.5) * samples / BANDS
        window = np.where(np.abs(away) <= half, np.exp(-0.5 * (away / (samples / 8)) ** 2), 0.0)
        norms.append(float(1.0 / np.sum(window * window)))
    edge = float(np.exp(-0.5 * (half / (samples / 8)) ** 2))
    return np.stack([even, odd]).astype(ml_dtypes.bfloat16), norms, edge


class Whole:
    def __init__(self, ref):
        self.ref = ref

    def __getitem__(self, at):
        return self.ref[at].astype(jnp.int32)


def maps_kernel(
    norms, edge, strips, step, count, outer, gives_edge, waits, near_tables, values, x_hbm, scale_ref,
    table_in, *refs,
):
    refs = list(refs)
    ext_ref = refs.pop(0) if outer[0] or outer[1] else None
    if waits:
        refs.pop(0)
    send_ref, keep_ref = refs.pop(0), refs.pop(0)
    give_ref = refs.pop(0) if gives_edge else None
    rough_ref, struct_ref, x_ref, level_ref, near_ref, sems = refs[:6]
    scratch = refs[6:]
    if not near_tables:
        table_ref = scratch.pop()
    lines = LANES
    samples = x_hbm.shape[-1]
    blocks = samples // LANES
    parts = lines // SUB
    rows = REPEATS * SUB
    info = Whole(values)
    flip = info[0]
    tile = jnp.where(flip == 1, count - 1 - step, step)
    lane = lax.broadcasted_iota(jnp.int32, (SUB, LANES), 1)
    mirror = jnp.where(lane == 0, 0, LANES - lane)
    sign = jnp.where(lane % 2 == 0, edge, -edge)

    line_count = x_hbm.shape[1]
    base = pl.multiple_of(tile * lines, lines)
    base_prev = pl.multiple_of(jnp.maximum(base - SUB, 0), SUB)
    base_next = pl.multiple_of(jnp.minimum(base + lines, line_count - SUB), SUB)
    first_copy = pltpu.make_async_copy(
        x_hbm.at[:, pl.ds(base, 2 * SUB), :], x_ref.at[:, : 2 * SUB, :], sems.at[0]
    )
    own = pltpu.make_async_copy(
        x_hbm.at[:, pl.ds(pl.multiple_of(base + 2 * SUB, SUB), lines - 2 * SUB), :],
        x_ref.at[:, 2 * SUB : lines, :],
        sems.at[5],
    )
    tables = []
    if near_tables:
        even_ref, odd_ref = table_in.at[0], table_in.at[1]
    else:
        even_ref, odd_ref = table_ref.at[0], table_ref.at[1]
        tables.append(pltpu.make_async_copy(table_in, table_ref, sems.at[1]))
    starts = [base_prev, base_next]
    if gives_edge:
        base_give = pl.multiple_of(jnp.where(flip == 1, 0, line_count - SUB), SUB)
        starts.append(base_give)
    edges = [
        pltpu.make_async_copy(x_hbm.at[:, pl.ds(start, SUB), :], near_ref.at[n], sems.at[(3, 4, 6)[n]])
        for n, start in enumerate(starts)
    ]
    for copy in [first_copy] + tables + edges + [own]:
        copy.start()

    at_start, at_end = tile == 0, tile == count - 1
    whole_prev = pl.ds(pl.multiple_of(jnp.maximum(base - lines, 0), lines), lines)
    whole_next = pl.ds(pl.multiple_of(jnp.minimum(base + lines, line_count - lines), lines), lines)

    def placed(values, at):
        above = jnp.zeros((at, values.shape[1]), values.dtype)
        below = jnp.zeros((SUB - 2 - at, values.shape[1]), values.dtype)
        return jnp.concatenate([piece for piece in (above, values, below) if piece.shape[0]], axis=0)

    row_of = lax.broadcasted_iota(jnp.int32, (SUB, blocks), 0)
    for r in range(REPEATS):
        level_ref[r, :lines, :] = scale_ref[r, :, pl.ds(base, lines)].T
        level_prev = scale_ref[r, :, whole_prev].T[lines - SUB :]
        level_next = scale_ref[r, :, whole_next].T[:SUB]
        if outer[0] or outer[1]:
            outside = ext_ref[2 * r : 2 * r + 2, samples : samples + blocks]
        if outer[0]:
            level_prev = jnp.where(at_start, placed(outside, SUB - 2), level_prev)
        if outer[1]:
            level_next = jnp.where(at_end, placed(outside, 0), level_next)
        level_ref[r, lines:, :] = jnp.where(row_of < 2, level_next, level_prev)

    def fold(s, buffers):
        even_in, odd_in, edge_in = buffers
        for r in range(REPEATS):
            at = pl.ds(pl.multiple_of(s * SUB, SUB), SUB)
            level = level_ref[r, at, :]
            values = [
                x_ref[r, at, kb * LANES : (kb + 1) * LANES].astype(jnp.float32)
                * level[:, kb : kb + 1]
                for kb in range(blocks)
            ]
            forward = [v.astype(jnp.bfloat16) for v in values]
            turned = [
                jnp.take_along_axis(v, mirror, axis=1, mode="promise_in_bounds") for v in values
            ]
            zero = jnp.zeros((SUB, LANES), jnp.float32)
            backward = []
            for i in range(blocks + 1):
                first = turned[blocks - i] if i > 0 else zero
                rest = turned[blocks - 1 - i] if i < blocks else zero
                backward.append(jnp.where(lane == 0, first, rest).astype(jnp.bfloat16))
            span = blocks // BANDS
            for band in range(BANDS):
                to = slice(band * rows + r * SUB, band * rows + r * SUB + SUB)
                centre = span // 2 + span * band
                for i in range(blocks // 2):
                    ahead = forward[centre + i] if centre + i < blocks else None
                    j = blocks - centre + i
                    behind = backward[j] if j <= blocks else None
                    if behind is None:
                        plus, minus = ahead, ahead
                    elif ahead is None:
                        plus, minus = behind, -behind
                    else:
                        plus, minus = ahead + behind, ahead - behind
                    even_in[to, i * LANES : (i + 1) * LANES] = plus
                    odd_in[to, i * LANES : (i + 1) * LANES] = minus
                far = centre + blocks // 2
                far = far if far < blocks else centre - blocks // 2
                edge_in[to, :] = forward[far].astype(jnp.float32)[:, :1] * sign

    def limits(t):
        return info[2 + 2 * t], info[3 + 2 * t]

    first, last = limits(tile)
    prev_first, prev_last = limits(jnp.maximum(tile - 1, 0))
    next_first, next_last = limits(jnp.minimum(tile + 1, count - 1))
    out_at = 2 + 4 * count
    prev_first = jnp.where(at_start, info[out_at] if outer[0] else 1 << 20, prev_first)
    prev_last = jnp.where(at_start, info[out_at + 1] if outer[0] else -1, prev_last)
    next_first = jnp.where(at_end, info[out_at + 2] if outer[1] else 1 << 20, next_first)
    next_last = jnp.where(at_end, info[out_at + 3] if outer[1] else -1, next_last)

    def shut(values, low, high, at=0):
        out = []
        for n in range(values.shape[1] // LANES):
            inside = jnp.logical_and(low <= at + n, at + n <= high)
            out.append(jnp.where(inside, values[:, n * LANES : (n + 1) * LANES], 0.0))
        return jnp.concatenate(out, axis=1)

    def finish(powers_of):
        ratio, total = None, None
        for band in range(BANDS):
            powers = [powers_of(band, r) for r in range(REPEATS)]
            level = (powers[0] + powers[1]) + (powers[2] + powers[3])
            level = level * (norms[band] / (BANDS * REPEATS))
            total = level if total is None else total + level
            for p, q in zip(powers[:-1], powers[1:]):
                product, both = p * q, p + q
                part = product * lax.rsqrt(product * (both * both))
                ratio = part if ratio is None else ratio + part
        rough = 1.0 - ratio * (2.0 / (BANDS * (REPEATS - 1)))
        return rough, jnp.log(total + 0.05)

    def dots(s, buffers, border):
        even_in, odd_in, edge_in = buffers
        wide = DEPTH // SPLIT

        def product(part, source, table):
            columns = slice(part * wide, (part + 1) * wide)
            return jnp.dot(source[...], table[:, columns], preferred_element_type=jnp.float32)

        def complete(part, re, im):
            columns = slice(part * wide, (part + 1) * wide)
            block0 = part * (wide // LANES)
            for g in range(SUB // 8):

                def power(band, r):
                    at = slice(band * rows + r * SUB + g * 8, band * rows + r * SUB + g * 8 + 8)
                    extra = jnp.concatenate([edge_in[at]] * (wide // LANES), axis=1)
                    a, b = re[at] + extra, im[at]
                    return a * a + b * b + 0.05 / norms[band]

                rough, struct = finish(power)
                if border:
                    rough_ref[g * 8 : g * 8 + 8, columns] = shut(rough, prev_first, prev_last, block0)
                    at = SUB + lines + g * 8
                    rough_ref[at : at + 8, columns] = shut(rough, next_first, next_last, block0)
                else:
                    line0 = pl.multiple_of(s * SUB + g * 8, 8)
                    rough_ref[pl.ds(line0 + SUB, 8), columns] = shut(rough, first, last, block0)
                    struct_ref[pl.ds(line0, 8), columns] = struct

        re0 = product(0, even_in, even_ref)
        im0 = product(0, odd_in, odd_ref)
        re1 = product(1, even_in, even_ref)
        complete(0, re0, im0)
        im1 = product(1, odd_in, odd_ref)
        complete(1, re1, im1)

    bufs = [scratch[0:3], scratch[3:6]]
    first_copy.wait()
    fold(0, bufs[0])
    for copy in tables:
        copy.wait()
    dots(0, bufs[0], False)
    fold(1, bufs[1])
    for copy in [own] + edges:
        copy.wait()
    for r in range(REPEATS):
        for kb in range(blocks):
            columns = slice(kb * LANES, (kb + 1) * LANES)
            a = near_ref[0, r, :, columns].astype(jnp.float32)
            b = near_ref[1, r, :, columns].astype(jnp.float32)
            if outer[0]:
                a = jnp.where(at_start, placed(ext_ref[2 * r : 2 * r + 2, columns], SUB - 2), a)
            if outer[1]:
                b = jnp.where(at_end, placed(ext_ref[2 * r : 2 * r + 2, columns], 0), b)
            low = lax.broadcasted_iota(jnp.int32, (SUB, LANES), 0) < 2
            x_ref[r, lines:, columns] = jnp.where(low, b, a).astype(jnp.bfloat16)

    if gives_edge:
        give_cols = pl.ds(pl.multiple_of(jnp.where(flip == 1, 0, line_count - lines), lines), lines)
        give_tile = jnp.where(flip == 1, 0, count - 1)
        for r in range(REPEATS):
            at = slice(2 * r, 2 * r + 2)
            for kb in range(blocks):
                columns = slice(kb * LANES, (kb + 1) * LANES)
                piece = near_ref[2, r, :, columns].astype(jnp.float32)
                give_ref[at, columns] = jnp.where(flip == 1, piece[:2], piece[SUB - 2 :])
            level = scale_ref[r, :, give_cols].T
            level = jnp.where(flip == 1, level[:2], level[lines - 2 :])
            edge_first = info[2 + 2 * give_tile].astype(jnp.float32)
            edge_last = info[3 + 2 * give_tile].astype(jnp.float32)
            give_ref[at, samples:] = jnp.concatenate(
                [
                    level,
                    jnp.full((2, 1), edge_first, jnp.float32),
                    jnp.full((2, 1), edge_last, jnp.float32),
                    jnp.zeros((2, LANES - blocks - 2), jnp.float32),
                ],
                axis=1,
            )


    def pair(i, carry):
        dots(2 * i + 1, bufs[1], False)
        fold(2 * i + 2, bufs[0])
        dots(2 * i + 2, bufs[0], False)
        fold(2 * i + 3, bufs[1])
        return carry

    lax.fori_loop(0, parts // 2 - 1, pair, 0)
    dots(parts - 1, bufs[1], False)
    fold(parts, bufs[0])
    dots(parts, bufs[0], True)

    pick = info[2 + 2 * count + tile]
    chosen = struct_ref[:, pl.ds(pl.multiple_of(pick * LANES, LANES), LANES)]
    score = jnp.sum(chosen) * (1.0 / (LANES * lines)) + values[2 + 3 * count + tile]
    smooth = TAPS[0] * rough_ref[SUB - 2 : SUB - 2 + lines, :]
    for k in range(1, 5):
        smooth = smooth + TAPS[k] * rough_ref[SUB - 2 + k : SUB - 2 + k + lines, :]
    maps = (smooth, shut(struct_ref[...], first, last))
    half = (send_ref.shape[0] - 8) // 2
    strip = DEPTH // strips
    low = info[1] % 2 == 0
    for m, whole in enumerate(maps):
        for zb in range(DEPTH // LANES):
            block = whole[:, zb * LANES : (zb + 1) * LANES].T
            for s in range(LANES // (2 * strip)):
                a = block[2 * s * strip : (2 * s + 1) * strip]
                b = block[(2 * s + 1) * strip : (2 * s + 2) * strip]
                at = m * half + zb * (LANES // 2) + s * strip
                keep_ref[at : at + strip, :] = jnp.where(low, a, b)
                send_ref[at : at + strip, :] = jnp.where(low, b, a)
    row = jnp.full((8, lines), score, jnp.float32)
    keep_ref[2 * half :, :] = row
    send_ref[2 * half :, :] = row


SUB = 16
MIB = 1024 * 1024
NEAR = (True, True, True)
LIMIT = (48 * MIB, 48 * MIB, 48 * MIB)
SPLIT = 2


def maps_call(step, count, outer, gives_edge, info, spectra, scales, extra, table, norms, edge, strips):
    samples = spectra.shape[-1]
    rows = BANDS * REPEATS * SUB
    out = jax.ShapeDtypeStruct((DEPTH + 8, LANES), jnp.float32)
    half = samples // 2
    whole = pl.BlockSpec(memory_space=pltpu.VMEM)
    remote = pl.BlockSpec(memory_space=pltpu.HBM)
    scales = jnp.swapaxes(scales, 1, 2)
    has_ext = outer[0] or outer[1]
    waits = len(extra) > has_ext
    outs = [out, out]
    if gives_edge:
        outs.append(jax.ShapeDtypeStruct((2 * REPEATS, samples + LANES), jnp.float32))
    pair = [
        pltpu.VMEM((rows, half), jnp.bfloat16),
        pltpu.VMEM((rows, half), jnp.bfloat16),
        pltpu.VMEM((rows, LANES), jnp.float32),
    ]
    scratch = [
        pltpu.VMEM((LANES + 2 * SUB, DEPTH), jnp.float32),
        pltpu.VMEM((LANES, DEPTH), jnp.float32),
        pltpu.VMEM((REPEATS, LANES + SUB, samples), jnp.bfloat16),
        pltpu.VMEM((REPEATS, LANES + SUB, samples // LANES), jnp.float32),
        pltpu.VMEM((3, REPEATS, SUB, samples), jnp.bfloat16),
        pltpu.SemaphoreType.DMA((7,)),
    ] + pair + pair
    near_tables = NEAR[step]
    if not near_tables:
        scratch.append(pltpu.VMEM((2, half, DEPTH), jnp.bfloat16))
    return pl.pallas_call(
        functools.partial(
            maps_kernel, norms, edge, strips, step, count, outer, gives_edge, waits, near_tables
        ),
        in_specs=[pl.BlockSpec(memory_space=pltpu.SMEM)]
        + [remote, whole, whole if near_tables else remote]
        + [whole] * has_ext + [pl.BlockSpec(memory_space=pl.ANY)] * waits,
        out_specs=[whole] * len(outs),
        scratch_shapes=scratch,
        out_shape=outs,
        compiler_params=pltpu.CompilerParams(vmem_limit_bytes=LIMIT[step]),
        cost_estimate=pl.CostEstimate(
            flops=5 * BANDS * REPEATS * (LANES + SUB) * samples * DEPTH,
            bytes_accessed=2 * REPEATS * LANES * samples + 4 * samples * DEPTH,
            transcendentals=0,
        ),
        name="maps",
    )(info, spectra, scales, table, *extra)


def merge_kernel(rows, strip, shares, tied, vol, keep_ref, recv_ref, *outs):
    outs = outs[len(outs) - shares - tied : len(outs) - tied]
    top_a, top_b = keep_ref[2 * rows : 2 * rows + 8], recv_ref[2 * rows : 2 * rows + 8]
    top = jnp.maximum(top_a, top_b)
    wa, wb = jnp.exp(top_a - top), jnp.exp(top_b - top)
    row = lax.broadcasted_iota(jnp.int32, (8, LANES), 0)
    tail = jnp.where(row < 4, top, wa + wb)
    wa, wb = wa[:1], wb[:1]
    mine = vol[0] // 2
    for d in range(shares):
        t = jnp.bitwise_xor(mine, d)
        at = pl.ds(pl.multiple_of(t * strip, strip), strip)
        struct = pl.ds(pl.multiple_of(rows + t * strip, strip), strip)
        sa, sb = keep_ref[at, :], recv_ref[at, :]
        first, other = wa * sa, wb * sb
        outs[d][:strip] = first + other
        outs[d][strip : 2 * strip] = first * sa + other * sb
        outs[d][2 * strip : 3 * strip] = wa * keep_ref[struct, :] + wb * recv_ref[struct, :]
        outs[d][3 * strip :] = tail


def merge_call(vol, keep, recv, later, strips):
    strip, shares = DEPTH // strips, strips // 2
    whole = pl.BlockSpec(memory_space=pltpu.VMEM)
    remote = pl.BlockSpec(memory_space=pl.ANY)
    out = jax.ShapeDtypeStruct((3 * strip + 8, LANES), jnp.float32)
    tied = [jax.ShapeDtypeStruct(a.shape, a.dtype) for a in later[:1]]
    return pl.pallas_call(
        functools.partial(merge_kernel, DEPTH // 2, strip, shares, len(tied)),
        in_specs=[pl.BlockSpec(memory_space=pltpu.SMEM), whole, whole] + [remote] * len(later),
        out_specs=[whole] * shares + [remote] * len(tied),
        out_shape=[out] * shares + tied,
        input_output_aliases={3: shares} if tied else {},
        compiler_params=pltpu.CompilerParams(vmem_limit_bytes=4 * 1024 * 1024),
        name="merge",
    )(vol, keep, recv, *later)


def final_kernel(strip, count, shares, info, *refs):
    parts, (angio_ref, joined_ref, spread_ref) = refs[: count * shares], refs[count * shares :]
    for i in range(count):
        mine = parts[i * shares : (i + 1) * shares]
        tops = [p[3 * strip : 3 * strip + 1] for p in mine]
        top = functools.reduce(jnp.maximum, tops)
        scales = [jnp.exp(t - top) for t in tops]
        weight = functools.reduce(
            lambda a, b: a + b, [w * p[3 * strip + 4 : 3 * strip + 5] for w, p in zip(scales, mine)]
        )
        scales = [w / weight for w in scales]
        mean, second, joined = (
            functools.reduce(
                lambda a, b: a + b,
                [w * p[m * strip : (m + 1) * strip] for w, p in zip(scales, mine)],
            )
            for m in range(3)
        )
        tile = jnp.where(info[0] == 1, count - 1 - i, i)
        columns = pl.ds(pl.multiple_of(tile * LANES, LANES), LANES)
        angio_ref[:, columns] = mean
        joined_ref[:, columns] = joined
        spread_ref[:, columns] = jnp.sqrt(second - mean * mean + 0.01)


def final_call(info, parts, count, strips):
    strip, shares = DEPTH // strips, strips // 2
    whole = pl.BlockSpec(memory_space=pltpu.VMEM)
    out = jax.ShapeDtypeStruct((strip, count * LANES), jnp.float32)
    return pl.pallas_call(
        functools.partial(final_kernel, strip, count, shares),
        in_specs=[pl.BlockSpec(memory_space=pltpu.SMEM)] + [whole] * len(parts),
        out_specs=[whole] * 3,
        out_shape=[out] * 3,
        compiler_params=pltpu.CompilerParams(vmem_limit_bytes=4 * 1024 * 1024),
        name="final",
    )(info, *parts)


def edge_rows(spectra, scales, start, block):
    lines = lax.dynamic_slice_in_dim(spectra, start, 2, axis=1).astype(jnp.float32)
    level = lax.dynamic_slice_in_dim(scales, start, 2, axis=1)
    rows = lines.shape[0] * 2
    limits = jnp.broadcast_to(block.astype(jnp.float32)[None], (rows, 2))
    rest = jnp.zeros((rows, LANES - level.shape[2] - 2), jnp.float32)
    return jnp.concatenate(
        [lines.reshape(rows, -1), level.reshape(rows, -1), limits, rest], axis=1
    )


def on_device(tiles, strips, spectra, scales, retina, quality, bias):
    spectra, scales, quality, bias = spectra[0], scales[0], quality[0], bias[0]
    samples = spectra.shape[-1]
    count = retina.shape[0]
    table, norms, edge = constants(samples)
    table = jnp.asarray(table)
    here = lax.axis_index("tile")
    vol = lax.axis_index("vol")
    lines = spectra.shape[1]

    at = samples + scales.shape[2]
    none = jnp.array([1 << 20, -1], jnp.float32)
    flip = (here == 1).astype(jnp.int32) if tiles == 2 else jnp.zeros((), jnp.int32)
    info = jnp.concatenate(
        [
            flip[None].astype(jnp.float32),
            vol[None].astype(jnp.float32),
            retina.reshape(-1).astype(jnp.float32),
            quality.astype(jnp.float32),
            bias,
        ]
    )

    def with_limits(before, after):
        before_block = jnp.where(here == 0, none, before[0, at : at + 2])
        after_block = jnp.where(here == tiles - 1, none, after[0, at : at + 2])
        return jnp.concatenate([info, before_block, after_block])

    if tiles == 2:
        outside = [(False, False)] * (count - 1) + [(True, True)]
    else:
        up = [(i, i + 1) for i in range(tiles - 1)]
        down = [(i + 1, i) for i in range(tiles - 1)]
        before = lax.ppermute(edge_rows(spectra, scales, lines - 2, retina[count - 1]), "tile", up)
        after = lax.ppermute(edge_rows(spectra, scales, 0, retina[0]), "tile", down)
        info = with_limits(before, after)
        outside = [(i == 0, i == count - 1) for i in range(count)]

    shares = strips // 2
    swap = [(v, v ^ 1) for v in range(strips)]
    kept, arrived, parts = [], [], []

    def merge(i, later):
        outs = merge_call(vol[None], kept[i], arrived[i], later, strips)
        got = [
            lax.ppermute(outs[d], "vol", [(v, v ^ (2 * d)) for v in range(strips)])
            for d in [*range(2, shares), 1][: shares - 1]
        ]
        parts.append([outs[0]] + got)
        return outs[-1]

    for i in range(count):
        outer = outside[i]
        gives_edge = tiles == 2 and i == 0
        extra = []
        if outer[0] or outer[1]:
            if tiles == 2:
                after = lax.ppermute(given, "tile", [(0, 1), (1, 0)])
                step_info = with_limits(after, after)
            else:
                step_info = info
            extra.append(after if outer[1] else before)
        else:
            step_info = info
        if i >= 2:
            if i == 2:
                merge(0, [])
            extra.append(parts[i - 2][0])
        send, keep, *rest = maps_call(
            i, count, outer, gives_edge, step_info,
            spectra, scales, extra, table, norms, edge, strips,
        )
        if gives_edge:
            given = rest[0]
        kept.append(keep)
        if i >= 2:
            send = merge(i - 1, [send] + parts[i - 2][1:])
        arrived.append(lax.ppermute(send, "vol", swap))
    for i in range(len(parts), count):
        merge(i, [])
    flat = [p for own in parts for p in own]
    return tuple(final_call(info, flat, count, strips))


def solution(mesh):
    return jax.shard_map(
        functools.partial(on_device, mesh.shape["tile"], mesh.shape["vol"]),
        mesh=mesh,
        in_specs=(
            P(("study", "vol"), None, "tile", None),
            P(("study", "vol"), None, "tile", None),
            P(("study", "tile"), None),
            P(("study", "vol"), "tile"),
            P(("study", "vol"), "tile"),
        ),
        out_specs=(P(("study", "vol"), "tile"),) * 3,
        check_vma=False,
    )
```

```python
import functools
import math

import jax
import jax.numpy as jnp
import ml_dtypes
import numpy as np
from jax import lax
from jax.experimental import pallas as pl
from jax.experimental.pallas import tpu as pltpu
from jax.sharding import PartitionSpec as P

DEPTH = 512
BANDS = 4
REPEATS = 4
LANES = 128
HALO = 8
TAPS = (1.0 / 9.0, 2.0 / 9.0, 3.0 / 9.0, 2.0 / 9.0, 1.0 / 9.0)


def constants(samples):
    half = samples // 2
    distance = np.arange(half, dtype=np.float64)
    gauss = np.exp(-0.5 * (distance / (samples / 8)) ** 2)
    turn = 2.0 * np.pi * ((np.arange(half)[:, None] * np.arange(DEPTH)[None, :]) % samples) / samples
    even = gauss[:, None] * np.cos(turn)
    even[0] *= 0.5
    odd = gauss[:, None] * np.sin(turn)
    norms = []
    for band in range(BANDS):
        away = np.arange(samples) - (band + 0.5) * samples / BANDS
        window = np.where(np.abs(away) <= half, np.exp(-0.5 * (away / (samples / 8)) ** 2), 0.0)
        norms.append(float(1.0 / np.sum(window * window)))
    edge = float(np.exp(-0.5 * (half / (samples / 8)) ** 2))
    return np.stack([even, odd]).astype(ml_dtypes.bfloat16), norms, edge


class Whole:
    def __init__(self, ref):
        self.ref = ref

    def __getitem__(self, at):
        return self.ref[at].astype(jnp.int32)


def maps_kernel(
    norms, edge, strips, step, count, outer, gives_edge, waits, near_tables, values, x_hbm, scale_ref,
    table_in, *refs,
):
    refs = list(refs)
    ext_ref = refs.pop(0) if outer[0] or outer[1] else None
    if waits:
        refs.pop(0)
    send_ref, keep_ref = refs.pop(0), refs.pop(0)
    give_ref = refs.pop(0) if gives_edge else None
    rough_ref, struct_ref, x_ref, level_ref, near_ref, sems = refs[:6]
    scratch = refs[6:]
    if not near_tables:
        table_ref = scratch.pop()
    lines = LANES
    samples = x_hbm.shape[-1]
    blocks = samples // LANES
    parts = lines // SUB
    rows = REPEATS * SUB
    info = Whole(values)
    flip = info[0]
    tile = jnp.where(flip == 1, count - 1 - step, step)
    lane = lax.broadcasted_iota(jnp.int32, (SUB, LANES), 1)
    mirror = jnp.where(lane == 0, 0, LANES - lane)
    sign = jnp.where(lane % 2 == 0, edge, -edge)

    line_count = x_hbm.shape[1]
    base = pl.multiple_of(tile * lines, lines)
    base_prev = pl.multiple_of(jnp.maximum(base - SUB, 0), SUB)
    base_next = pl.multiple_of(jnp.minimum(base + lines, line_count - SUB), SUB)
    first_copy = pltpu.make_async_copy(
        x_hbm.at[:, pl.ds(base, 2 * SUB), :], x_ref.at[:, : 2 * SUB, :], sems.at[0]
    )
    own = pltpu.make_async_copy(
        x_hbm.at[:, pl.ds(pl.multiple_of(base + 2 * SUB, SUB), lines - 2 * SUB), :],
        x_ref.at[:, 2 * SUB : lines, :],
        sems.at[5],
    )
    tables = []
    if near_tables:
        even_ref, odd_ref = table_in.at[0], table_in.at[1]
    else:
        even_ref, odd_ref = table_ref.at[0], table_ref.at[1]
        tables.append(pltpu.make_async_copy(table_in, table_ref, sems.at[1]))
    starts = [base_prev, base_next]
    if gives_edge:
        base_give = pl.multiple_of(jnp.where(flip == 1, 0, line_count - SUB), SUB)
        starts.append(base_give)
    edges = [
        pltpu.make_async_copy(x_hbm.at[:, pl.ds(start, SUB), :], near_ref.at[n], sems.at[(3, 4, 6)[n]])
        for n, start in enumerate(starts)
    ]
    for copy in [first_copy] + tables + edges + [own]:
        copy.start()

    at_start, at_end = tile == 0, tile == count - 1
    whole_prev = pl.ds(pl.multiple_of(jnp.maximum(base - lines, 0), lines), lines)
    whole_next = pl.ds(pl.multiple_of(jnp.minimum(base + lines, line_count - lines), lines), lines)

    def placed(values, at):
        above = jnp.zeros((at, values.shape[1]), values.dtype)
        below = jnp.zeros((SUB - 2 - at, values.shape[1]), values.dtype)
        return jnp.concatenate([piece for piece in (above, values, below) if piece.shape[0]], axis=0)

    row_of = lax.broadcasted_iota(jnp.int32, (SUB, blocks), 0)
    for r in range(REPEATS):
        level_ref[r, :lines, :] = scale_ref[r, :, pl.ds(base, lines)].T
        level_prev = scale_ref[r, :, whole_prev].T[lines - SUB :]
        level_next = scale_ref[r, :, whole_next].T[:SUB]
        if outer[0] or outer[1]:
            outside = ext_ref[2 * r : 2 * r + 2, samples : samples + blocks]
        if outer[0]:
            level_prev = jnp.where(at_start, placed(outside, SUB - 2), level_prev)
        if outer[1]:
            level_next = jnp.where(at_end, placed(outside, 0), level_next)
        level_ref[r, lines:, :] = jnp.where(row_of < 2, level_next, level_prev)

    def fold(s, buffers):
        even_in, odd_in, edge_in = buffers
        for r in range(REPEATS):
            at = pl.ds(pl.multiple_of(s * SUB, SUB), SUB)
            level = level_ref[r, at, :]
            values = [
                x_ref[r, at, kb * LANES : (kb + 1) * LANES].astype(jnp.float32)
                * level[:, kb : kb + 1]
                for kb in range(blocks)
            ]
            forward = [v.astype(jnp.bfloat16) for v in values]
            turned = [
                jnp.take_along_axis(v, mirror, axis=1, mode="promise_in_bounds") for v in values
            ]
            zero = jnp.zeros((SUB, LANES), jnp.float32)
            backward = []
            for i in range(blocks + 1):
                first = turned[blocks - i] if i > 0 else zero
                rest = turned[blocks - 1 - i] if i < blocks else zero
                backward.append(jnp.where(lane == 0, first, rest).astype(jnp.bfloat16))
            span = blocks // BANDS
            for band in range(BANDS):
                to = slice(band * rows + r * SUB, band * rows + r * SUB + SUB)
                centre = span // 2 + span * band
                for i in range(blocks // 2):
                    ahead = forward[centre + i] if centre + i < blocks else None
                    j = blocks - centre + i
                    behind = backward[j] if j <= blocks else None
                    if behind is None:
                        plus, minus = ahead, ahead
                    elif ahead is None:
                        plus, minus = behind, -behind
                    else:
                        plus, minus = ahead + behind, ahead - behind
                    even_in[to, i * LANES : (i + 1) * LANES] = plus
                    odd_in[to, i * LANES : (i + 1) * LANES] = minus
                far = centre + blocks // 2
                far = far if far < blocks else centre - blocks // 2
                edge_in[to, :] = forward[far].astype(jnp.float32)[:, :1] * sign

    def limits(t):
        return info[2 + 2 * t], info[3 + 2 * t]

    first, last = limits(tile)
    prev_first, prev_last = limits(jnp.maximum(tile - 1, 0))
    next_first, next_last = limits(jnp.minimum(tile + 1, count - 1))
    out_at = 2 + 4 * count
    prev_first = jnp.where(at_start, info[out_at] if outer[0] else 1 << 20, prev_first)
    prev_last = jnp.where(at_start, info[out_at + 1] if outer[0] else -1, prev_last)
    next_first = jnp.where(at_end, info[out_at + 2] if outer[1] else 1 << 20, next_first)
    next_last = jnp.where(at_end, info[out_at + 3] if outer[1] else -1, next_last)

    def shut(values, low, high, at=0):
        out = []
        for n in range(values.shape[1] // LANES):
            inside = jnp.logical_and(low <= at + n, at + n <= high)
            out.append(jnp.where(inside, values[:, n * LANES : (n + 1) * LANES], 0.0))
        return jnp.concatenate(out, axis=1)

    def finish(powers_of):
        ratio, total = None, None
        for band in range(BANDS):
            powers = [powers_of(band, r) for r in range(REPEATS)]
            level = (powers[0] + powers[1]) + (powers[2] + powers[3])
            level = level * (norms[band] / (BANDS * REPEATS))
            total = level if total is None else total + level
            for p, q in zip(powers[:-1], powers[1:]):
                product, both = p * q, p + q
                part = product * lax.rsqrt(product * (both * both))
                ratio = part if ratio is None else ratio + part
        rough = 1.0 - ratio * (2.0 / (BANDS * (REPEATS - 1)))
        return rough, jnp.log(total + 0.05)

    def dots(s, buffers, border):
        even_in, odd_in, edge_in = buffers
        wide = DEPTH // SPLIT

        def product(part, source, table):
            columns = slice(part * wide, (part + 1) * wide)
            return jnp.dot(source[...], table[:, columns], preferred_element_type=jnp.float32)

        def complete(part, re, im):
            columns = slice(part * wide, (part + 1) * wide)
            block0 = part * (wide // LANES)
            for g in range(SUB // 8):

                def power(band, r):
                    at = slice(band * rows + r * SUB + g * 8, band * rows + r * SUB + g * 8 + 8)
                    extra = jnp.concatenate([edge_in[at]] * (wide // LANES), axis=1)
                    a, b = re[at] + extra, im[at]
                    return a * a + b * b + 0.05 / norms[band]

                rough, struct = finish(power)
                if border:
                    rough_ref[g * 8 : g * 8 + 8, columns] = shut(rough, prev_first, prev_last, block0)
                    at = SUB + lines + g * 8
                    rough_ref[at : at + 8, columns] = shut(rough, next_first, next_last, block0)
                else:
                    line0 = pl.multiple_of(s * SUB + g * 8, 8)
                    rough_ref[pl.ds(line0 + SUB, 8), columns] = shut(rough, first, last, block0)
                    struct_ref[pl.ds(line0, 8), columns] = struct

        re0 = product(0, even_in, even_ref)
        im0 = product(0, odd_in, odd_ref)
        re1 = product(1, even_in, even_ref)
        complete(0, re0, im0)
        im1 = product(1, odd_in, odd_ref)
        complete(1, re1, im1)

    bufs = [scratch[0:3], scratch[3:6]]
    first_copy.wait()
    fold(0, bufs[0])
    for copy in tables:
        copy.wait()
    dots(0, bufs[0], False)
    fold(1, bufs[1])
    own.wait()

    def pair(i, carry):
        dots(2 * i + 1, bufs[1], False)
        fold(2 * i + 2, bufs[0])
        dots(2 * i + 2, bufs[0], False)
        fold(2 * i + 3, bufs[1])
        return carry

    lax.fori_loop(0, parts // 2 - 1, pair, 0)
    for copy in edges:
        copy.wait()
    dots(parts - 1, bufs[1], False)
    for r in range(REPEATS):
        for kb in range(blocks):
            columns = slice(kb * LANES, (kb + 1) * LANES)
            a = near_ref[0, r, :, columns].astype(jnp.float32)
            b = near_ref[1, r, :, columns].astype(jnp.float32)
            if outer[0]:
                a = jnp.where(at_start, placed(ext_ref[2 * r : 2 * r + 2, columns], SUB - 2), a)
            if outer[1]:
                b = jnp.where(at_end, placed(ext_ref[2 * r : 2 * r + 2, columns], 0), b)
            low = lax.broadcasted_iota(jnp.int32, (SUB, LANES), 0) < 2
            x_ref[r, lines:, columns] = jnp.where(low, b, a).astype(jnp.bfloat16)

    if gives_edge:
        give_cols = pl.ds(pl.multiple_of(jnp.where(flip == 1, 0, line_count - lines), lines), lines)
        give_tile = jnp.where(flip == 1, 0, count - 1)
        for r in range(REPEATS):
            at = slice(2 * r, 2 * r + 2)
            for kb in range(blocks):
                columns = slice(kb * LANES, (kb + 1) * LANES)
                piece = near_ref[2, r, :, columns].astype(jnp.float32)
                give_ref[at, columns] = jnp.where(flip == 1, piece[:2], piece[SUB - 2 :])
            level = scale_ref[r, :, give_cols].T
            level = jnp.where(flip == 1, level[:2], level[lines - 2 :])
            edge_first = info[2 + 2 * give_tile].astype(jnp.float32)
            edge_last = info[3 + 2 * give_tile].astype(jnp.float32)
            give_ref[at, samples:] = jnp.concatenate(
                [
                    level,
                    jnp.full((2, 1), edge_first, jnp.float32),
                    jnp.full((2, 1), edge_last, jnp.float32),
                    jnp.zeros((2, LANES - blocks - 2), jnp.float32),
                ],
                axis=1,
            )
    fold(parts, bufs[0])
    dots(parts, bufs[0], True)

    pick = info[2 + 2 * count + tile]
    chosen = struct_ref[:, pl.ds(pl.multiple_of(pick * LANES, LANES), LANES)]
    score = jnp.sum(chosen) * (1.0 / (LANES * lines)) + values[2 + 3 * count + tile]
    smooth = TAPS[0] * rough_ref[SUB - 2 : SUB - 2 + lines, :]
    for k in range(1, 5):
        smooth = smooth + TAPS[k] * rough_ref[SUB - 2 + k : SUB - 2 + k + lines, :]
    maps = (smooth, shut(struct_ref[...], first, last))
    half = (send_ref.shape[0] - 8) // 2
    strip = DEPTH // strips
    low = info[1] % 2 == 0
    for m, whole in enumerate(maps):
        for zb in range(DEPTH // LANES):
            block = whole[:, zb * LANES : (zb + 1) * LANES].T
            for s in range(LANES // (2 * strip)):
                a = block[2 * s * strip : (2 * s + 1) * strip]
                b = block[(2 * s + 1) * strip : (2 * s + 2) * strip]
                at = m * half + zb * (LANES // 2) + s * strip
                keep_ref[at : at + strip, :] = jnp.where(low, a, b)
                send_ref[at : at + strip, :] = jnp.where(low, b, a)
    row = jnp.full((8, lines), score, jnp.float32)
    keep_ref[2 * half :, :] = row
    send_ref[2 * half :, :] = row


SUB = 16
MIB = 1024 * 1024
NEAR = (True, True, True)
LIMIT = (48 * MIB, 48 * MIB, 48 * MIB)
SPLIT = 2


def maps_call(step, count, outer, gives_edge, info, spectra, scales, extra, table, norms, edge, strips):
    samples = spectra.shape[-1]
    rows = BANDS * REPEATS * SUB
    out = jax.ShapeDtypeStruct((DEPTH + 8, LANES), jnp.float32)
    half = samples // 2
    whole = pl.BlockSpec(memory_space=pltpu.VMEM)
    remote = pl.BlockSpec(memory_space=pltpu.HBM)
    scales = jnp.swapaxes(scales, 1, 2)
    has_ext = outer[0] or outer[1]
    waits = len(extra) > has_ext
    outs = [out, out]
    if gives_edge:
        outs.append(jax.ShapeDtypeStruct((2 * REPEATS, samples + LANES), jnp.float32))
    pair = [
        pltpu.VMEM((rows, half), jnp.bfloat16),
        pltpu.VMEM((rows, half), jnp.bfloat16),
        pltpu.VMEM((rows, LANES), jnp.float32),
    ]
    scratch = [
        pltpu.VMEM((LANES + 2 * SUB, DEPTH), jnp.float32),
        pltpu.VMEM((LANES, DEPTH), jnp.float32),
        pltpu.VMEM((REPEATS, LANES + SUB, samples), jnp.bfloat16),
        pltpu.VMEM((REPEATS, LANES + SUB, samples // LANES), jnp.float32),
        pltpu.VMEM((3, REPEATS, SUB, samples), jnp.bfloat16),
        pltpu.SemaphoreType.DMA((7,)),
    ] + pair + pair
    near_tables = NEAR[step]
    if not near_tables:
        scratch.append(pltpu.VMEM((2, half, DEPTH), jnp.bfloat16))
    return pl.pallas_call(
        functools.partial(
            maps_kernel, norms, edge, strips, step, count, outer, gives_edge, waits, near_tables
        ),
        in_specs=[pl.BlockSpec(memory_space=pltpu.SMEM)]
        + [remote, whole, whole if near_tables else remote]
        + [whole] * has_ext + [pl.BlockSpec(memory_space=pl.ANY)] * waits,
        out_specs=[whole] * len(outs),
        scratch_shapes=scratch,
        out_shape=outs,
        compiler_params=pltpu.CompilerParams(vmem_limit_bytes=LIMIT[step]),
        cost_estimate=pl.CostEstimate(
            flops=5 * BANDS * REPEATS * (LANES + SUB) * samples * DEPTH,
            bytes_accessed=2 * REPEATS * LANES * samples + 4 * samples * DEPTH,
            transcendentals=0,
        ),
        name="maps",
    )(info, spectra, scales, table, *extra)


def merge_kernel(rows, strip, shares, tied, vol, keep_ref, recv_ref, *outs):
    outs = outs[len(outs) - shares - tied : len(outs) - tied]
    top_a, top_b = keep_ref[2 * rows : 2 * rows + 8], recv_ref[2 * rows : 2 * rows + 8]
    top = jnp.maximum(top_a, top_b)
    wa, wb = jnp.exp(top_a - top), jnp.exp(top_b - top)
    row = lax.broadcasted_iota(jnp.int32, (8, LANES), 0)
    tail = jnp.where(row < 4, top, wa + wb)
    wa, wb = wa[:1], wb[:1]
    mine = vol[0] // 2
    for d in range(shares):
        t = jnp.bitwise_xor(mine, d)
        at = pl.ds(pl.multiple_of(t * strip, strip), strip)
        struct = pl.ds(pl.multiple_of(rows + t * strip, strip), strip)
        sa, sb = keep_ref[at, :], recv_ref[at, :]
        first, other = wa * sa, wb * sb
        outs[d][:strip] = first + other
        outs[d][strip : 2 * strip] = first * sa + other * sb
        outs[d][2 * strip : 3 * strip] = wa * keep_ref[struct, :] + wb * recv_ref[struct, :]
        outs[d][3 * strip :] = tail


def merge_call(vol, keep, recv, later, strips):
    strip, shares = DEPTH // strips, strips // 2
    whole = pl.BlockSpec(memory_space=pltpu.VMEM)
    remote = pl.BlockSpec(memory_space=pl.ANY)
    out = jax.ShapeDtypeStruct((3 * strip + 8, LANES), jnp.float32)
    tied = [jax.ShapeDtypeStruct(a.shape, a.dtype) for a in later[:1]]
    return pl.pallas_call(
        functools.partial(merge_kernel, DEPTH // 2, strip, shares, len(tied)),
        in_specs=[pl.BlockSpec(memory_space=pltpu.SMEM), whole, whole] + [remote] * len(later),
        out_specs=[whole] * shares + [remote] * len(tied),
        out_shape=[out] * shares + tied,
        input_output_aliases={3: shares} if tied else {},
        compiler_params=pltpu.CompilerParams(vmem_limit_bytes=4 * 1024 * 1024),
        name="merge",
    )(vol, keep, recv, *later)


def final_kernel(strip, count, shares, info, *refs):
    parts, (angio_ref, joined_ref, spread_ref) = refs[: count * shares], refs[count * shares :]
    for i in range(count):
        mine = parts[i * shares : (i + 1) * shares]
        tops = [p[3 * strip : 3 * strip + 1] for p in mine]
        top = functools.reduce(jnp.maximum, tops)
        scales = [jnp.exp(t - top) for t in tops]
        weight = functools.reduce(
            lambda a, b: a + b, [w * p[3 * strip + 4 : 3 * strip + 5] for w, p in zip(scales, mine)]
        )
        scales = [w / weight for w in scales]
        mean, second, joined = (
            functools.reduce(
                lambda a, b: a + b,
                [w * p[m * strip : (m + 1) * strip] for w, p in zip(scales, mine)],
            )
            for m in range(3)
        )
        tile = jnp.where(info[0] == 1, count - 1 - i, i)
        columns = pl.ds(pl.multiple_of(tile * LANES, LANES), LANES)
        angio_ref[:, columns] = mean
        joined_ref[:, columns] = joined
        spread_ref[:, columns] = jnp.sqrt(second - mean * mean + 0.01)


def final_call(info, parts, count, strips):
    strip, shares = DEPTH // strips, strips // 2
    whole = pl.BlockSpec(memory_space=pltpu.VMEM)
    out = jax.ShapeDtypeStruct((strip, count * LANES), jnp.float32)
    return pl.pallas_call(
        functools.partial(final_kernel, strip, count, shares),
        in_specs=[pl.BlockSpec(memory_space=pltpu.SMEM)] + [whole] * len(parts),
        out_specs=[whole] * 3,
        out_shape=[out] * 3,
        compiler_params=pltpu.CompilerParams(vmem_limit_bytes=4 * 1024 * 1024),
        name="final",
    )(info, *parts)


def edge_rows(spectra, scales, start, block):
    lines = lax.dynamic_slice_in_dim(spectra, start, 2, axis=1).astype(jnp.float32)
    level = lax.dynamic_slice_in_dim(scales, start, 2, axis=1)
    rows = lines.shape[0] * 2
    limits = jnp.broadcast_to(block.astype(jnp.float32)[None], (rows, 2))
    rest = jnp.zeros((rows, LANES - level.shape[2] - 2), jnp.float32)
    return jnp.concatenate(
        [lines.reshape(rows, -1), level.reshape(rows, -1), limits, rest], axis=1
    )


def on_device(tiles, strips, spectra, scales, retina, quality, bias):
    spectra, scales, quality, bias = spectra[0], scales[0], quality[0], bias[0]
    samples = spectra.shape[-1]
    count = retina.shape[0]
    table, norms, edge = constants(samples)
    table = jnp.asarray(table)
    here = lax.axis_index("tile")
    vol = lax.axis_index("vol")
    lines = spectra.shape[1]

    at = samples + scales.shape[2]
    none = jnp.array([1 << 20, -1], jnp.float32)
    flip = (here == 1).astype(jnp.int32) if tiles == 2 else jnp.zeros((), jnp.int32)
    info = jnp.concatenate(
        [
            flip[None].astype(jnp.float32),
            vol[None].astype(jnp.float32),
            retina.reshape(-1).astype(jnp.float32),
            quality.astype(jnp.float32),
            bias,
        ]
    )

    def with_limits(before, after):
        before_block = jnp.where(here == 0, none, before[0, at : at + 2])
        after_block = jnp.where(here == tiles - 1, none, after[0, at : at + 2])
        return jnp.concatenate([info, before_block, after_block])

    if tiles == 2:
        outside = [(False, False)] * (count - 1) + [(True, True)]
    else:
        up = [(i, i + 1) for i in range(tiles - 1)]
        down = [(i + 1, i) for i in range(tiles - 1)]
        before = lax.ppermute(edge_rows(spectra, scales, lines - 2, retina[count - 1]), "tile", up)
        after = lax.ppermute(edge_rows(spectra, scales, 0, retina[0]), "tile", down)
        info = with_limits(before, after)
        outside = [(i == 0, i == count - 1) for i in range(count)]

    shares = strips // 2
    swap = [(v, v ^ 1) for v in range(strips)]
    kept, arrived, parts = [], [], []

    def merge(i, later):
        outs = merge_call(vol[None], kept[i], arrived[i], later, strips)
        got = [
            lax.ppermute(outs[d], "vol", [(v, v ^ (2 * d)) for v in range(strips)])
            for d in [*range(2, shares), 1][: shares - 1]
        ]
        parts.append([outs[0]] + got)
        return outs[-1]

    for i in range(count):
        outer = outside[i]
        gives_edge = tiles == 2 and i == 0
        extra = []
        if outer[0] or outer[1]:
            if tiles == 2:
                after = lax.ppermute(given, "tile", [(0, 1), (1, 0)])
                step_info = with_limits(after, after)
            else:
                step_info = info
            extra.append(after if outer[1] else before)
        else:
            step_info = info
        if i >= 2:
            if i == 2:
                merge(0, [])
            extra.append(parts[i - 2][0])
        send, keep, *rest = maps_call(
            i, count, outer, gives_edge, step_info,
            spectra, scales, extra, table, norms, edge, strips,
        )
        if gives_edge:
            given = rest[0]
        kept.append(keep)
        if i >= 2:
            send = merge(i - 1, [send] + parts[i - 2][1:])
        arrived.append(lax.ppermute(send, "vol", swap))
    for i in range(len(parts), count):
        merge(i, [])
    flat = [p for own in parts for p in own]
    return tuple(final_call(info, flat, count, strips))


def solution(mesh):
    return jax.shard_map(
        functools.partial(on_device, mesh.shape["tile"], mesh.shape["vol"]),
        mesh=mesh,
        in_specs=(
            P(("study", "vol"), None, "tile", None),
            P(("study", "vol"), None, "tile", None),
            P(("study", "tile"), None),
            P(("study", "vol"), "tile"),
            P(("study", "vol"), "tile"),
        ),
        out_specs=(P(("study", "vol"), "tile"),) * 3,
        check_vma=False,
    )
```
